32 devices in a mesh: lon: 8 (over y, x, core), lat: 4 (over z).
Axes of the slice: x: 2, y: 2, z: 4, core: 2. Of those that a mesh axis runs over, the one named last changes fastest.
Arguments:
- state_prev: float32 [7, 16, 64, 1024], P(None, None, 'lat', 'lon'), may hold values from -6 to 6
- state_now: float32 [7, 16, 64, 1024], P(None, None, 'lat', 'lon'), may hold values from -6 to 6
- stride_table: int32 [64], P('lat'), may hold values from 1 to 32, as said below
- filter_len: int32 [64], P('lat'), may hold values from 1 to 32, as said below
- zonal_coef: float32 [64], P('lat'), may hold values from 0.05 to 0.3
- merid_coef: float32 [16], replicated, may hold values from 0.05 to 0.3
- filter_coef: float32 [16], replicated, may hold values from 0.03 to 0.2
- w_first: bfloat16 [7, 64], replicated, may hold values from -2 to 2
- b_first: float32 [64], replicated, may hold values from -3 to 3
- w_second: bfloat16 [64, 64], replicated, may hold values from -0.75 to 0.75
- b_second: float32 [64], replicated, may hold values from -3 to 3
- w_third: bfloat16 [64, 224], replicated, may hold values from -0.75 to 0.75
- b_third: float32 [224], replicated, may hold values from -3 to 3
- band_weight: float32 [224], replicated, may hold values from 0.02 to 0.2
- sunlit_cols: int32 [4, 8, 1536], P('lat', 'lon'), may hold values from 0 to 2047, as said below
- sunlit_count: int32 [4, 8], P('lat'), may hold values from 0 to 1536, as said below
Outputs:
- prev_out: float32 [7, 16, 64, 1024], P(None, None, 'lat', 'lon')
- now_out: float32 [7, 16, 64, 1024], P(None, None, 'lat', 'lon')
The draws below stay inside these ranges and needn't reach their ends.
Inputs may be any that keep to these rules, and one draw needn't show every extreme that they name: `stride_table`: 1 except in the 4 rows nearest each end of the latitude range. `filter_len`: 1 except in the 4 rows nearest each end of the latitude range. `sunlit_cols`: the entries of one device's list are distinct. `sunlit_count`: a device's count plus that of the device 8 / 2 further along lon (cyclic) in the same band is at most 1536.
All inputs are finite; a program needn't handle non-finite values.
Results may differ from the reference program's by a relative error of at most 0.0003.
Values may be sent and summed in bfloat16 or wider, within the bound.
A program may use at most 64 MiB of HBM per device.

```python
import math
import jax
import jax.numpy as jnp
from jax import lax

CLON = 128
CLAT = 16
LEV = 16
VARS = 7
HID = 64
GPT = 224
SMAX = 32
POLAR = 4
RCOL = 1536
NLON = 1024
NLAT = 64
N_LON = 8
N_LAT = 4


def polar_table(key, salt):
    rows = jnp.arange(NLAT, dtype=jnp.int32)
    dist = jnp.minimum(rows, NLAT - 1 - rows)
    values = jax.random.randint(jax.random.fold_in(key, salt), (NLAT,), 1, SMAX + 1, dtype=jnp.int32)
    values = jnp.where(dist == 0, SMAX, values)
    return jnp.where(dist < POLAR, values, 1).astype(jnp.int32)


def draw_stride_table(key, part):
    return polar_table(key, 11)


def draw_filter_len(key, part):
    return polar_table(key, 23)


def draw_sunlit_cols(key, part):
    keys = jax.random.split(jax.random.fold_in(key, 37), N_LAT * N_LON)
    lists = jax.vmap(lambda k: jax.random.permutation(k, CLAT * CLON)[:RCOL])(keys)
    return lists.reshape(N_LAT, N_LON, RCOL).astype(jnp.int32)


def draw_sunlit_count(key, part):
    half = N_LON // 2
    base = jax.random.fold_in(key, 53)
    day = jax.random.randint(jax.random.fold_in(base, 1), (N_LAT, half), RCOL // 2, RCOL + 1, dtype=jnp.int32)
    pairs = jnp.arange(half, dtype=jnp.int32)
    day = jnp.where(pairs[None, :] == 0, RCOL, day)
    spare = RCOL - day
    night = jax.random.randint(jax.random.fold_in(base, 2), (N_LAT, half), 0, RCOL + 1, dtype=jnp.int32) % (spare + 1)
    flip = jax.random.randint(jax.random.fold_in(base, 3), (N_LAT, half), 0, 2, dtype=jnp.int32)
    first = jnp.where(flip == 1, day, night)
    second = jnp.where(flip == 1, night, day)
    return jnp.concatenate([first, second], axis=1).astype(jnp.int32)


def steps_of(rng, dims, cuts, low, high):
    gain, own = 1.0, jax.random.fold_in(rng, 6)
    for position, parts in cuts:
        draws = jnp.exp(jax.random.uniform(jax.random.fold_in(own, position), (parts,), jnp.float32, low / len(cuts), high / len(cuts)))
        gain = gain * jnp.repeat(draws, dims[position] // parts).reshape([-1 if axis == position else 1 for axis in range(len(dims))])
    return gain


def bell_draw(stream_key, shape, spread, most, cuts=(), kind=jnp.bfloat16):
    array = spread * jax.random.normal(stream_key, shape, jnp.float32)
    if cuts:
        array = array * steps_of(stream_key, shape, cuts, -0.22, 0.18)
    return jnp.clip(array, -most, most).astype(kind)


def setup_inputs(seed: int = 0) -> dict:
    arg_keys = jax.random.split(jax.random.key(seed), 17)
    return {
        "state_prev": bell_draw(arg_keys[0], (VARS, LEV, NLAT, NLON), 1.0, 6.0, ((2, 4), (3, 8)), jnp.float32),
        "state_now": bell_draw(arg_keys[1], (VARS, LEV, NLAT, NLON), 1.0, 6.0, ((2, 4), (3, 8)), jnp.float32),
        "stride_table": draw_stride_table(jax.random.fold_in(arg_keys[16], 71), 0),
        "filter_len": draw_filter_len(jax.random.fold_in(arg_keys[16], 71), 0),
        "zonal_coef": jnp.clip(jnp.exp(math.log(0.3) - 1.7917595 * jax.random.uniform(arg_keys[4], (NLAT,), jnp.float32) ** steps_of(arg_keys[4], (NLAT,), ((0, 4),), -0.2, 0.2)), 0.05, 0.3),
        "merid_coef": jnp.clip(jnp.exp(jax.random.uniform(arg_keys[5], (LEV,), jnp.float32, math.log(0.05), math.log(0.3))), 0.05, 0.3),
        "filter_coef": jnp.clip(jnp.exp(jax.random.uniform(arg_keys[6], (LEV,), jnp.float32, math.log(0.03), math.log(0.2))), 0.03, 0.2),
        "w_first": bell_draw(arg_keys[7], (VARS, HID), VARS ** -0.5, 2.0),
        "b_first": bell_draw(arg_keys[8], (HID,), 0.5, 3.0, (), jnp.float32),
        "w_second": bell_draw(arg_keys[9], (HID, HID), HID ** -0.5, 0.75),
        "b_second": bell_draw(arg_keys[10], (HID,), 0.5, 3.0, (), jnp.float32),
        "w_third": bell_draw(arg_keys[11], (HID, GPT), HID ** -0.5, 0.75),
        "b_third": bell_draw(arg_keys[12], (GPT,), 0.5, 3.0, (), jnp.float32),
        "band_weight": jnp.clip(jnp.exp(jax.random.uniform(arg_keys[13], (GPT,), jnp.float32, math.log(0.02), math.log(0.2))), 0.02, 0.2),
        "sunlit_cols": draw_sunlit_cols(jax.random.fold_in(arg_keys[16], 71), 0),
        "sunlit_count": draw_sunlit_count(jax.random.fold_in(arg_keys[16], 71), 0),
    }


def absorb(feats_t, w_first, b_first, w_second, b_second, w_third, b_third, band_weight):
    count = feats_t.shape[2]
    levels = feats_t.shape[1]
    rows = jnp.transpose(feats_t, (2, 1, 0)).reshape(count * levels, feats_t.shape[0])
    first = jax.nn.silu(jnp.dot(rows, w_first, preferred_element_type=jnp.float32) + b_first).astype(jnp.bfloat16)
    second = jax.nn.silu(jnp.dot(first, w_second, preferred_element_type=jnp.float32) + b_second).astype(jnp.bfloat16)
    tau = 0.15 * jax.nn.softplus(jnp.dot(second, w_third, preferred_element_type=jnp.float32) + b_third)
    tau = tau.reshape(count, levels, tau.shape[-1])
    depth = jnp.cumsum(tau, axis=1)
    above = depth - tau
    return jnp.sum((jnp.exp(-above) - jnp.exp(-depth)) * band_weight, axis=-1)


def step(prev, now, stride_table, filter_len, zonal_coef, merid_coef, filter_coef):
    width = now.shape[-1]
    cols = jnp.arange(width, dtype=jnp.int32)
    inv_s = 1.0 / stride_table.astype(jnp.float32)
    wind_u = now[0]
    wind_v = now[1]

    def pick(field, offset):
        index = (cols[None, :] + offset[:, None]) % width
        return jnp.take_along_axis(field, jnp.broadcast_to(index[None], field.shape), axis=2)

    def advance(pair):
        old, field = pair
        plus = pick(field, stride_table)
        minus = pick(field, -stride_table)
        fplus = pick(field, filter_len)
        fminus = pick(field, -filter_len)
        padded = jnp.pad(field, ((0, 0), (1, 1), (0, 0)))
        merid = padded[:, 2:] - padded[:, :-2]
        tend = -zonal_coef[None, :, None] * wind_u * ((plus - minus) * inv_s[None, :, None])
        tend = tend - merid_coef[:, None, None] * wind_v * merid
        tend = tend + filter_coef[:, None, None] * (fplus - 2.0 * field + fminus)
        return old + tend

    new = lax.map(advance, (prev, now))
    return now + 0.1 * (prev - 2.0 * now + new), new


def reference(state_prev, state_now, stride_table, filter_len, zonal_coef, merid_coef, filter_coef, w_first, b_first, w_second, b_second, w_third, b_third, band_weight, sunlit_cols, sunlit_count):
    prev, now = state_prev, state_now
    for turn in range(2):
        prev, now = step(prev, now, stride_table, filter_len, zonal_coef, merid_coef, filter_coef)
    devices = N_LAT * N_LON
    listed = sunlit_cols.reshape(devices, RCOL).astype(jnp.int32)
    which = jnp.arange(devices, dtype=jnp.int32)
    glat = (which // N_LON)[:, None] * CLAT + listed // CLON
    glon = (which % N_LON)[:, None] * CLON + listed % CLON
    counts = sunlit_count.reshape(devices).astype(jnp.int32)
    slots = jnp.arange(RCOL, dtype=jnp.int32)

    def one(args):
        rows_here, cols_here, live = args
        feats = now[:, :, rows_here, cols_here].astype(jnp.bfloat16)
        heat = absorb(feats, w_first, b_first, w_second, b_second, w_third, b_third, band_weight)
        return jnp.where((slots < live)[:, None], heat, jnp.float32(0.0))

    heats = lax.map(one, (glat, glon, counts))
    temper = now[2].at[:, glat.reshape(-1), glon.reshape(-1)].add(heats.reshape(-1, LEV).T)
    now_out = now.at[2].set(temper)
    return prev, now_out
```

```python
import functools
import math

import jax
import jax.numpy as jnp
from jax import lax
from jax.experimental import pallas as pl
from jax.experimental.pallas import tpu as pltpu
from jax.sharding import PartitionSpec as P

SMAX = 32
POLAR = 4
MESH = pl.DeviceIdType.MESH
LOG2E = math.log2(math.e)
RATE = 0.15


def column(row, lanes):
    return jnp.transpose(jnp.broadcast_to(row, (lanes, row.shape[1])))


def flipped(weight):
    rows = weight.shape[0]
    eye = (
        lax.broadcasted_iota(jnp.int32, (rows, rows), 0)
        == lax.broadcasted_iota(jnp.int32, (rows, rows), 1)
    ).astype(jnp.float32).astype(jnp.bfloat16)
    return lax.dot_general(
        weight, eye, (((0,), (0,)), ((), ())), preferred_element_type=jnp.float32
    )


def kernel(
    dims,
    prev_ref,
    now_ref,
    stride_ref,
    flen_ref,
    zcoef_ref,
    count_ref,
    mcoef_ref,
    fcoef_ref,
    w1_ref,
    b1_ref,
    w2_ref,
    b2_ref,
    w3_ref,
    b3_ref,
    band_ref,
    list_ref,
    prev_out,
    now_out,
    now0,
    now1,
    prev1,
    temper,
    feats,
    lon_out,
    lon_in,
    lat_in,
    w1big,
    w2t,
    w3t,
    bias1,
    bias2,
    bias3,
    start3,
    first,
    second,
    depth,
    heat,
    mask,
    send_sem,
    recv_sem,
):
    nvar, lev, rows, lanes, n_lon, n_lat = dims
    hid = w2_ref.shape[0]
    gpt = w3_ref.shape[1]
    lon = lax.axis_index("lon")
    lat = lax.axis_index("lat")
    east = lax.rem(lon + 1, n_lon)
    west = lax.rem(lon + n_lon - 1, n_lon)
    at_top = lat == 0
    at_end = lat == n_lat - 1
    polar = jnp.logical_or(at_top, at_end)
    pstart = jnp.where(at_top, 0, rows - POLAR)
    body_lo = jnp.where(at_top, POLAR, 0)
    body_hi = jnp.where(at_end, rows - POLAR, rows)

    barrier = pltpu.get_barrier_semaphore()
    for peer in (east, west):
        pl.semaphore_signal(barrier, inc=1, device_id={"lon": peer}, device_id_type=MESH)

    @pl.when(lat > 0)
    def _():
        pl.semaphore_signal(barrier, inc=1, device_id={"lat": lat - 1}, device_id_type=MESH)

    @pl.when(lat < n_lat - 1)
    def _():
        pl.semaphore_signal(barrier, inc=1, device_id={"lat": lat + 1}, device_id_type=MESH)

    lane = lax.broadcasted_iota(jnp.int32, (lev, lanes), 1)

    def zonal(turn, side, whole):
        part = pl.ds(0, nvar + 1) if whole else pl.ds(nvar, 1)
        return pltpu.make_async_remote_copy(
            src_ref=lon_out.at[turn, side, part],
            dst_ref=lon_in.at[turn, side, part],
            send_sem=send_sem.at[turn, side],
            recv_sem=recv_sem.at[turn, side],
            device_id={"lon": west if side == 0 else east},
            device_id_type=MESH,
        )

    def merid_copy(turn, side, src):
        return pltpu.make_async_remote_copy(
            src_ref=src.at[:, 1 if side == 0 else rows],
            dst_ref=lat_in.at[turn, side],
            send_sem=send_sem.at[turn, 2 + side],
            recv_sem=recv_sem.at[turn, 2 + side],
            device_id={"lat": lat - 1 if side == 0 else lat + 1},
            device_id_type=MESH,
        )

    def send_rows(turn, src):
        @pl.when(lat > 0)
        def _():
            merid_copy(turn, 0, src).start()

        @pl.when(lat < n_lat - 1)
        def _():
            merid_copy(turn, 1, src).start()

    def send_sides(turn, src):
        def gather_edges(j, edges):
            head, tail = edges
            for v in range(nvar):
                x = src[v, j + 1]
                place = v * rows + j
                head = jnp.where(lane == place, pltpu.roll(x, place, 1), head)
                tail = jnp.where(lane == place, pltpu.roll(x, lax.rem(place + 1, lanes), 1), tail)
            return head, tail

        zero = jnp.zeros((lev, lanes), jnp.float32)
        head, tail = lax.fori_loop(0, rows, gather_edges, (zero, zero))
        lon_out[turn, 0, nvar] = head
        lon_out[turn, 1, nvar] = tail

        @pl.when(polar)
        def _():
            for v in range(nvar):
                head = jnp.zeros((lev, lanes), jnp.float32)
                tail = head
                for q in range(POLAR):
                    x = src[v, pstart + q + 1]
                    here = lane // SMAX == q
                    head = jnp.where(here, pltpu.roll(x, (SMAX * q) % lanes, 1), head)
                    tail = jnp.where(here, pltpu.roll(x, (SMAX * q + SMAX) % lanes, 1), tail)
                lon_out[turn, 0, v] = head
                lon_out[turn, 1, v] = tail
            zonal(turn, 0, True).start()
            zonal(turn, 1, True).start()

        @pl.when(jnp.logical_not(polar))
        def _():
            zonal(turn, 0, False).start()
            zonal(turn, 1, False).start()

    def finish(turn, src):
        @pl.when(polar)
        def _():
            zonal(turn, 0, True).wait()
            zonal(turn, 1, True).wait()

        @pl.when(jnp.logical_not(polar))
        def _():
            zonal(turn, 0, False).wait()
            zonal(turn, 1, False).wait()

        @pl.when(lat > 0)
        def _():
            merid_copy(turn, 0, src).wait_send()
            merid_copy(turn, 1, src).wait_recv()
            for v in range(nvar):
                src[v, 0] = lat_in[turn, 1, v]

        @pl.when(lat < n_lat - 1)
        def _():
            merid_copy(turn, 1, src).wait_send()
            merid_copy(turn, 0, src).wait_recv()
            for v in range(nvar):
                src[v, rows + 1] = lat_in[turn, 0, v]

        zero = jnp.zeros((lev, lanes), jnp.float32)

        @pl.when(at_top)
        def _():
            for v in range(nvar):
                src[v, 0] = zero

        @pl.when(at_end)
        def _():
            for v in range(nvar):
                src[v, rows + 1] = zero

    def leap(turn, src, get_prev, put):
        mcoef = column(mcoef_ref[...], lanes)
        fcoef = column(fcoef_ref[...], lanes)
        from_east = lon_in.at[turn, 0]
        from_west = lon_in.at[turn, 1]

        def emit(v, j, x, diff, ends, zu, mv):
            tend = zu * diff - mv * (src[v, j + 2] - src[v, j])
            tend = tend + fcoef * (ends - 2.0 * x)
            old = get_prev(v, j)
            new = old + tend
            put(v, j, x + 0.1 * (old - 2.0 * x + new), new)

        def plain(j, carry):
            zu = -zcoef_ref[j] * src[0, j + 1]
            mv = mcoef * src[1, j + 1]
            pe = from_east[nvar]
            pw = from_west[nvar]
            for v in range(nvar):
                x = src[v, j + 1]
                place = v * rows + j
                plus = jnp.where(
                    lane == lanes - 1,
                    pltpu.roll(pe, lanes - 1 - place, 1),
                    pltpu.roll(x, lanes - 1, 1),
                )
                minus = jnp.where(
                    lane == 0, pltpu.roll(pw, lax.rem(lanes - place, lanes), 1), pltpu.roll(x, 1, 1)
                )
                emit(v, j, x, plus - minus, plus + minus, zu, mv)
            return carry

        lax.fori_loop(body_lo, body_hi, plain, 0)

        @pl.when(polar)
        def _():
            for q in range(POLAR):
                j = pstart + q
                s = stride_ref[j]
                m = flen_ref[j]
                inv = 1.0 / jnp.full((lev, lanes), s, jnp.int32).astype(jnp.float32)
                zu = (-zcoef_ref[j] * src[0, j + 1])
                mv = mcoef * src[1, j + 1]
                for v in range(nvar):
                    x = src[v, j + 1]
                    he = pltpu.roll(from_east[v], (lanes - SMAX * q) % lanes, 1)
                    hw = pltpu.roll(from_west[v], (lanes - SMAX - SMAX * q) % lanes, 1)
                    pair = []
                    for n in (s, m):
                        plus = pltpu.roll(jnp.where(lane < n, he, x), lanes - n, 1)
                        minus = pltpu.roll(jnp.where(lane >= lanes - n, hw, x), n, 1)
                        pair.append((plus, minus))
                    diff = (pair[0][0] - pair[0][1]) * inv
                    emit(v, j, x, diff, pair[1][0] + pair[1][1], zu, mv)

    def load(j, carry):
        for v in range(nvar):
            now0[v, j + 1] = now_ref[v, pl.ds(j, lev, stride=rows), :]
        return carry

    lax.fori_loop(0, rows, load, 0)
    pl.semaphore_wait(
        barrier, 2 + jnp.where(lat > 0, 1, 0) + jnp.where(lat < n_lat - 1, 1, 0)
    )

    send_rows(0, now0)
    send_sides(0, now0)

    expand = (
        lax.broadcasted_iota(jnp.int32, (nvar, nvar * lev), 1) // lev
        == lax.broadcasted_iota(jnp.int32, (nvar, nvar * lev), 0)
    ).astype(jnp.float32).astype(jnp.bfloat16)
    spread = lax.dot_general(
        w1_ref[...], expand, (((0,), (0,)), ((), ())), preferred_element_type=jnp.float32
    )
    level = lax.broadcasted_iota(jnp.int32, (hid, nvar * lev), 1) % lev
    for k in range(lev):
        w1big[pl.ds(k * hid, hid), :] = jnp.where(level == k, spread, 0.0).astype(jnp.bfloat16)
    w2t[...] = flipped(w2_ref[...]).astype(jnp.bfloat16)
    w3t[...] = flipped(w3_ref[...]).astype(jnp.bfloat16)
    bias1[...] = column(0.5 * b1_ref[...], 2 * lanes)
    bias2[...] = column(0.5 * b2_ref[...], 2 * lanes)
    bias3[...] = column(LOG2E * b3_ref[...], 2 * lanes)
    start3[...] = column(jnp.log2(band_ref[...]) * (-1.0 / RATE), 2 * lanes)
    listed = list_ref[...]
    slots = listed.shape[1]
    live = lax.broadcasted_iota(jnp.int32, (1, slots), 1) < count_ref[0, lon]
    row_hot = jnp.logical_and(
        lax.broadcasted_iota(jnp.int32, (rows, slots), 0) == listed // lanes, live
    ).astype(jnp.float32).astype(jnp.bfloat16)
    lane_hot = (
        lax.broadcasted_iota(jnp.int32, (lanes, slots), 0) == listed % lanes
    ).astype(jnp.float32).astype(jnp.bfloat16)
    mask[...] = lax.dot_general(
        row_hot, lane_hot, (((1,), (1,)), ((), ())), preferred_element_type=jnp.float32
    )

    finish(0, now0)

    def put_first(v, j, filtered, new):
        prev1[v, j] = filtered
        now1[v, j + 1] = new

    leap(0, now0, lambda v, j: prev_ref[v, pl.ds(j, lev, stride=rows), :], put_first)
    send_rows(1, now1)
    send_sides(1, now1)
    finish(1, now1)

    def put_second(v, j, filtered, new):
        prev_out[v, pl.ds(j, lev, stride=rows), :] = filtered
        feats[j, pl.ds(v * lev, lev), :] = new.astype(jnp.bfloat16)
        if v == 2:
            temper[j] = new
        else:
            now_out[v, pl.ds(j, lev, stride=rows), :] = new

    leap(1, now1, lambda v, j: prev1[v, j], put_second)

    wide = 2 * lanes
    chunk = 16

    def absorb(pair, carry):
        cells = jnp.concatenate([feats[2 * pair], feats[2 * pair + 1]], axis=1)
        for k in range(lev):
            part = pl.ds(k * hid, hid)
            half = 0.5 * jnp.dot(w1big[part, :], cells, preferred_element_type=jnp.float32) + bias1[...]
            first[part, :] = (half + half * jnp.tanh(half)).astype(jnp.bfloat16)
        for k in range(lev):
            part = pl.ds(k * hid, hid)
            half = 0.5 * jnp.dot(w2t[...], first[part, :], preferred_element_type=jnp.float32) + bias2[...]
            second[part, :] = (half + half * jnp.tanh(half)).astype(jnp.bfloat16)
        depth[...] = start3[...]
        top = jnp.zeros((8, wide), jnp.float32)
        for g in range(0, gpt, 8):
            top = top + jnp.exp2(-RATE * start3[pl.ds(g, 8), :])

        def one_level(k, above):
            part = pl.ds(pl.multiple_of(k * hid, hid), hid)
            raw = jnp.dot(w3t[...], second[part, :], preferred_element_type=jnp.float32)
            total = jnp.zeros((8, wide), jnp.float32)
            for g in range(0, gpt, chunk):
                at = pl.ds(g, chunk)
                y = raw[g : g + chunk] * LOG2E + bias3[at, :]
                soft = jnp.maximum(y, jnp.log2(1.0 + jnp.exp2(jnp.minimum(y, 64.0))))
                here = depth[at, :] + soft
                depth[at, :] = here
                left = jnp.exp2(-RATE * here)
                for piece in range(0, chunk, 8):
                    total = total + left[piece : piece + 8]
            heat[pl.ds(k, 1), :] = jnp.sum(above - total, axis=0, keepdims=True)
            return total

        lax.fori_loop(0, lev, one_level, top, unroll=4)
        for side in range(2):
            j = 2 * pair + side
            warm = heat[:, side * lanes : (side + 1) * lanes] * mask[pl.ds(j, 1), :]
            now_out[2, pl.ds(j, lev, stride=rows), :] = temper[j] + warm
        return carry

    lax.fori_loop(0, rows // 2, absorb, 0)


def body(
    state_prev,
    state_now,
    stride_table,
    filter_len,
    zonal_coef,
    merid_coef,
    filter_coef,
    w_first,
    b_first,
    w_second,
    b_second,
    w_third,
    b_third,
    band_weight,
    sunlit_cols,
    sunlit_count,
):
    nvar, lev, rows, lanes = state_now.shape
    dims = (nvar, lev, rows, lanes, lax.axis_size("lon"), lax.axis_size("lat"))
    hid = w_second.shape[0]
    gpt = w_third.shape[1]
    flat = (nvar, lev * rows, lanes)
    vmem = pl.BlockSpec(memory_space=pltpu.VMEM)
    smem = pl.BlockSpec(memory_space=pltpu.SMEM)
    f32, bf16 = jnp.float32, jnp.bfloat16
    tile = (lev, lanes)
    shape = jax.ShapeDtypeStruct(flat, f32)
    prev, now = pl.pallas_call(
        functools.partial(kernel, dims),
        out_shape=(shape, shape),
        in_specs=[vmem] * 2 + [smem] * 4 + [vmem] * 10,
        out_specs=(vmem, vmem),
        scratch_shapes=[
            pltpu.VMEM((nvar, rows + 2) + tile, f32),
            pltpu.VMEM((nvar, rows + 2) + tile, f32),
            pltpu.VMEM((nvar, rows) + tile, f32),
            pltpu.VMEM((rows,) + tile, f32),
            pltpu.VMEM((rows, nvar * lev, lanes), bf16),
            pltpu.VMEM((2, 2, nvar + 1) + tile, f32),
            pltpu.VMEM((2, 2, nvar + 1) + tile, f32),
            pltpu.VMEM((2, 2, nvar) + tile, f32),
            pltpu.VMEM((lev * hid, nvar * lev), bf16),
            pltpu.VMEM((hid, hid), bf16),
            pltpu.VMEM((gpt, hid), bf16),
            pltpu.VMEM((hid, 2 * lanes), f32),
            pltpu.VMEM((hid, 2 * lanes), f32),
            pltpu.VMEM((gpt, 2 * lanes), f32),
            pltpu.VMEM((gpt, 2 * lanes), f32),
            pltpu.VMEM((lev * hid, 2 * lanes), bf16),
            pltpu.VMEM((lev * hid, 2 * lanes), bf16),
            pltpu.VMEM((gpt, 2 * lanes), f32),
            pltpu.VMEM((lev, 2 * lanes), f32),
            pltpu.VMEM((rows, lanes), f32),
            pltpu.SemaphoreType.DMA((2, 4)),
            pltpu.SemaphoreType.DMA((2, 4)),
        ],
        compiler_params=pltpu.CompilerParams(
            collective_id=0, has_side_effects=True, vmem_limit_bytes=40 * 1024 * 1024
        ),
    )(
        state_prev.reshape(flat),
        state_now.reshape(flat),
        stride_table,
        filter_len,
        zonal_coef,
        sunlit_count,
        merid_coef[None],
        filter_coef[None],
        w_first,
        b_first[None],
        w_second,
        b_second[None],
        w_third,
        b_third[None],
        band_weight[None],
        sunlit_cols.reshape(1, -1),
    )
    return prev.reshape(state_prev.shape), now.reshape(state_now.shape)


def solution(mesh):
    field = P(None, None, "lat", "lon")
    in_specs = (
        (field, field, P("lat"), P("lat"), P("lat"))
        + (P(),) * 9
        + (P("lat", "lon", None), P("lat", None))
    )
    return jax.shard_map(
        body, mesh=mesh, in_specs=in_specs, out_specs=(field, field), check_vma=False
    )
```

```python
import functools
import math

import jax
import jax.numpy as jnp
from jax import lax
from jax.experimental import pallas as pl
from jax.experimental.pallas import tpu as pltpu
from jax.sharding import PartitionSpec as P

SMAX = 32
POLAR = 4
MESH = pl.DeviceIdType.MESH
LOG2E = math.log2(math.e)
RATE = 0.15


def column(row, lanes):
    return jnp.transpose(jnp.broadcast_to(row, (lanes, row.shape[1])))


def flipped(weight):
    rows = weight.shape[0]
    eye = (
        lax.broadcasted_iota(jnp.int32, (rows, rows), 0)
        == lax.broadcasted_iota(jnp.int32, (rows, rows), 1)
    ).astype(jnp.float32).astype(jnp.bfloat16)
    return lax.dot_general(
        weight, eye, (((0,), (0,)), ((), ())), preferred_element_type=jnp.float32
    )


def kernel(dims, n_in, *refs):
    operands, refs = refs[:n_in], refs[n_in:]
    prev_out, now_out, refs = refs[0], refs[1], refs[2:]
    held, refs = refs[:n_in], refs[n_in:]
    (
        prev_ref,
        now_ref,
        stride_ref,
        flen_ref,
        zcoef_ref,
        count_ref,
        mcoef_ref,
        fcoef_ref,
        w1_ref,
        b1_ref,
        w2_ref,
        b2_ref,
        w3_ref,
        b3_ref,
        band_ref,
        list_ref,
    ) = held
    (
        now0,
        now1,
        prev1,
        temper,
        feats,
        lon_out,
        lon_in,
        lat_in,
        w1big,
        w2t,
        w3t,
        bias1,
        bias2,
        bias3,
        start3,
        first,
        second,
        depth,
        heat,
        hot,
        own,
        gone,
        come,
        heat_in,
        grid,
        load_sem,
        send_sem,
        recv_sem,
        far_send,
        far_recv,
    ) = refs
    nvar, lev, rows, lanes, n_lon, n_lat = dims
    hid = w2_ref.shape[0]
    gpt = w3_ref.shape[1]
    lon = lax.axis_index("lon")
    lat = lax.axis_index("lat")
    east = lax.rem(lon + 1, n_lon)
    west = lax.rem(lon + n_lon - 1, n_lon)
    far = lax.rem(lon + n_lon // 2, n_lon)
    at_top = lat == 0
    at_end = lat == n_lat - 1
    polar = jnp.logical_or(at_top, at_end)
    pstart = jnp.where(at_top, 0, rows - POLAR)
    body_lo = jnp.where(at_top, POLAR, 0)
    body_hi = jnp.where(at_end, rows - POLAR, rows)

    loads = [
        pltpu.make_async_copy(src, dst, load_sem.at[i])
        for i, (src, dst) in enumerate(zip(operands, held))
    ]
    for i in (1, *range(2, n_in), 0):
        loads[i].start()

    barrier = pltpu.get_barrier_semaphore()
    for peer in (east, west, far):
        pl.semaphore_signal(barrier, inc=1, device_id={"lon": peer}, device_id_type=MESH)

    @pl.when(lat > 0)
    def _():
        pl.semaphore_signal(barrier, inc=1, device_id={"lat": lat - 1}, device_id_type=MESH)

    @pl.when(lat < n_lat - 1)
    def _():
        pl.semaphore_signal(barrier, inc=1, device_id={"lat": lat + 1}, device_id_type=MESH)

    lane = lax.broadcasted_iota(jnp.int32, (lev, lanes), 1)

    def zonal(turn, side, whole):
        part = pl.ds(0, nvar + 1) if whole else pl.ds(nvar, 1)
        return pltpu.make_async_remote_copy(
            src_ref=lon_out.at[turn, side, part],
            dst_ref=lon_in.at[turn, side, part],
            send_sem=send_sem.at[turn, side],
            recv_sem=recv_sem.at[turn, side],
            device_id={"lon": west if side == 0 else east},
            device_id_type=MESH,
        )

    def merid_copy(turn, side, src):
        return pltpu.make_async_remote_copy(
            src_ref=src.at[:, 1 if side == 0 else rows],
            dst_ref=lat_in.at[turn, side],
            send_sem=send_sem.at[turn, 2 + side],
            recv_sem=recv_sem.at[turn, 2 + side],
            device_id={"lat": lat - 1 if side == 0 else lat + 1},
            device_id_type=MESH,
        )

    def send_rows(turn, src):
        @pl.when(lat > 0)
        def _():
            merid_copy(turn, 0, src).start()

        @pl.when(lat < n_lat - 1)
        def _():
            merid_copy(turn, 1, src).start()

    def send_sides(turn, src):
        def gather_edges(j, edges):
            head, tail = edges
            for v in range(nvar):
                x = src[v, j + 1]
                place = v * rows + j
                head = jnp.where(lane == place, pltpu.roll(x, place, 1), head)
                tail = jnp.where(lane == place, pltpu.roll(x, lax.rem(place + 1, lanes), 1), tail)
            return head, tail

        zero = jnp.zeros((lev, lanes), jnp.float32)
        head, tail = lax.fori_loop(0, rows, gather_edges, (zero, zero))
        lon_out[turn, 0, nvar] = head
        lon_out[turn, 1, nvar] = tail

        @pl.when(polar)
        def _():
            for v in range(nvar):
                head = jnp.zeros((lev, lanes), jnp.float32)
                tail = head
                for q in range(POLAR):
                    x = src[v, pstart + q + 1]
                    here = lane // SMAX == q
                    head = jnp.where(here, pltpu.roll(x, (SMAX * q) % lanes, 1), head)
                    tail = jnp.where(here, pltpu.roll(x, (SMAX * q + SMAX) % lanes, 1), tail)
                lon_out[turn, 0, v] = head
                lon_out[turn, 1, v] = tail
            zonal(turn, 0, True).start()
            zonal(turn, 1, True).start()

        @pl.when(jnp.logical_not(polar))
        def _():
            zonal(turn, 0, False).start()
            zonal(turn, 1, False).start()

    def finish(turn, src):
        @pl.when(polar)
        def _():
            zonal(turn, 0, True).wait()
            zonal(turn, 1, True).wait()

        @pl.when(jnp.logical_not(polar))
        def _():
            zonal(turn, 0, False).wait()
            zonal(turn, 1, False).wait()

        @pl.when(lat > 0)
        def _():
            merid_copy(turn, 0, src).wait_send()
            merid_copy(turn, 1, src).wait_recv()
            for v in range(nvar):
                src[v, 0] = lat_in[turn, 1, v]

        @pl.when(lat < n_lat - 1)
        def _():
            merid_copy(turn, 1, src).wait_send()
            merid_copy(turn, 0, src).wait_recv()
            for v in range(nvar):
                src[v, rows + 1] = lat_in[turn, 0, v]

        zero = jnp.zeros((lev, lanes), jnp.float32)

        @pl.when(at_top)
        def _():
            for v in range(nvar):
                src[v, 0] = zero

        @pl.when(at_end)
        def _():
            for v in range(nvar):
                src[v, rows + 1] = zero

    def leap(turn, src, get_prev, put):
        mcoef = column(mcoef_ref[...], lanes)
        fcoef = column(fcoef_ref[...], lanes)
        from_east = lon_in.at[turn, 0]
        from_west = lon_in.at[turn, 1]

        def emit(v, j, x, diff, ends, zu, mv):
            tend = zu * diff - mv * (src[v, j + 2] - src[v, j])
            tend = tend + fcoef * (ends - 2.0 * x)
            old = get_prev(v, j)
            new = old + tend
            put(v, j, x + 0.1 * (old - 2.0 * x + new), new)

        def plain(j, carry):
            zu = -zcoef_ref[j] * src[0, j + 1]
            mv = mcoef * src[1, j + 1]
            pe = from_east[nvar]
            pw = from_west[nvar]
            for v in range(nvar):
                x = src[v, j + 1]
                place = v * rows + j
                plus = jnp.where(
                    lane == lanes - 1,
                    pltpu.roll(pe, lanes - 1 - place, 1),
                    pltpu.roll(x, lanes - 1, 1),
                )
                minus = jnp.where(
                    lane == 0, pltpu.roll(pw, lax.rem(lanes - place, lanes), 1), pltpu.roll(x, 1, 1)
                )
                emit(v, j, x, plus - minus, plus + minus, zu, mv)
            return carry

        lax.fori_loop(body_lo, body_hi, plain, 0)

        @pl.when(polar)
        def _():
            for q in range(POLAR):
                j = pstart + q
                s = stride_ref[j]
                m = flen_ref[j]
                inv = 1.0 / jnp.full((lev, lanes), s, jnp.int32).astype(jnp.float32)
                zu = (-zcoef_ref[j] * src[0, j + 1])
                mv = mcoef * src[1, j + 1]
                for v in range(nvar):
                    x = src[v, j + 1]
                    he = pltpu.roll(from_east[v], (lanes - SMAX * q) % lanes, 1)
                    hw = pltpu.roll(from_west[v], (lanes - SMAX - SMAX * q) % lanes, 1)
                    pair = []
                    for n in (s, m):
                        plus = pltpu.roll(jnp.where(lane < n, he, x), lanes - n, 1)
                        minus = pltpu.roll(jnp.where(lane >= lanes - n, hw, x), n, 1)
                        pair.append((plus, minus))
                    diff = (pair[0][0] - pair[0][1]) * inv
                    emit(v, j, x, diff, pair[1][0] + pair[1][1], zu, mv)

    def load(j, carry):
        for v in range(nvar):
            now0[v, j + 1] = now_ref[v, pl.ds(j, lev, stride=rows), :]
        return carry

    loads[1].wait()
    lax.fori_loop(0, rows, load, 0)
    pl.semaphore_wait(
        barrier, 3 + jnp.where(lat > 0, 1, 0) + jnp.where(lat < n_lat - 1, 1, 0)
    )

    send_rows(0, now0)
    send_sides(0, now0)

    for i in (*range(2, n_in), 0):
        loads[i].wait()

    expand = (
        lax.broadcasted_iota(jnp.int32, (nvar, nvar * lev), 1) // lev
        == lax.broadcasted_iota(jnp.int32, (nvar, nvar * lev), 0)
    ).astype(jnp.float32).astype(jnp.bfloat16)
    spread = lax.dot_general(
        w1_ref[...], expand, (((0,), (0,)), ((), ())), preferred_element_type=jnp.float32
    )
    level = lax.broadcasted_iota(jnp.int32, (hid, nvar * lev), 1) % lev
    for k in range(lev):
        w1big[pl.ds(k * hid, hid), :] = jnp.where(level == k, spread, 0.0).astype(jnp.bfloat16)
    w2t[...] = flipped(w2_ref[...]).astype(jnp.bfloat16)
    w3t[...] = flipped(w3_ref[...]).astype(jnp.bfloat16)
    bias1[...] = column(0.5 * b1_ref[...], 2 * lanes)
    bias2[...] = column(0.5 * b2_ref[...], 2 * lanes)
    bias3[...] = column(LOG2E * b3_ref[...], 2 * lanes)
    start3[...] = column(jnp.log2(band_ref[...]) * (-1.0 / RATE), 2 * lanes)
    half = list_ref.shape[1] // 2
    mine = count_ref[0, lon]
    other = count_ref[0, far]
    slot = lax.broadcasted_iota(jnp.int32, (8, half), 1)
    shift = jnp.minimum(other, half - 1)
    moved = pltpu.roll(jnp.broadcast_to(list_ref[:, half:], (8, half)), shift, 1)
    for side, (cols, live) in enumerate(
        (
            (jnp.broadcast_to(list_ref[:, :half], (8, half)), slot < mine),
            (moved, jnp.logical_and(slot >= other, slot < other + mine - half)),
        )
    ):
        cols = jnp.where(live, cols, -1)[:1]
        at = pl.ds(side * half, half)
        lane_hot = (
            lax.broadcasted_iota(jnp.int32, (lanes, half), 0) == cols % lanes
        ).astype(jnp.float32).astype(jnp.bfloat16)
        for j in range(rows):
            row_hot = (cols // lanes == j).astype(jnp.float32).astype(jnp.bfloat16)
            hot[pl.ds(j * lanes, lanes), at] = lane_hot * row_hot

    finish(0, now0)

    def put_first(v, j, filtered, new):
        prev1[v, j] = filtered
        now1[v, j + 1] = new

    leap(0, now0, lambda v, j: prev_ref[v, pl.ds(j, lev, stride=rows), :], put_first)
    send_rows(1, now1)
    send_sides(1, now1)
    finish(1, now1)

    def put_second(v, j, filtered, new):
        prev_out[v, pl.ds(j, lev, stride=rows), :] = filtered
        at = pl.ds(pl.multiple_of(j * lanes, lanes), lanes)
        feats[pl.ds(v * lev, lev), at] = new.astype(jnp.bfloat16)
        if v == 2:
            temper[j] = new
        else:
            now_out[v, pl.ds(j, lev, stride=rows), :] = new

    leap(1, now1, lambda v, j: prev1[v, j], put_second)

    wide = 2 * lanes
    chunk = 16
    blocks = half // wide

    def picked(at):
        got = jnp.dot(feats[...], hot[:, pl.ds(at, wide)], preferred_element_type=jnp.float32)
        return got.astype(jnp.bfloat16)

    def to_far(b):
        return pltpu.make_async_remote_copy(
            src_ref=gone.at[b],
            dst_ref=come.at[b],
            send_sem=far_send.at[0, b],
            recv_sem=far_recv.at[0, b],
            device_id={"lon": far},
            device_id_type=MESH,
        )

    def back(b):
        return pltpu.make_async_remote_copy(
            src_ref=heat.at[b],
            dst_ref=heat_in.at[b],
            send_sem=far_send.at[1, b],
            recv_sem=far_recv.at[1, b],
            device_id={"lon": far},
            device_id_type=MESH,
        )

    for b in range(blocks):
        gone[b] = picked(half + b * wide)
        to_far(b).start()
    for b in range(blocks):
        own[b] = picked(b * wide)

    def absorb(b, carry):
        to_far(b).wait()
        cells = own[b] + come[b]
        for k in range(lev):
            part = pl.ds(k * hid, hid)
            x = 0.5 * jnp.dot(w1big[part, :], cells, preferred_element_type=jnp.float32) + bias1[...]
            first[part, :] = (x + x * jnp.tanh(x)).astype(jnp.bfloat16)
        for k in range(lev):
            part = pl.ds(k * hid, hid)
            x = 0.5 * jnp.dot(w2t[...], first[part, :], preferred_element_type=jnp.float32) + bias2[...]
            second[part, :] = (x + x * jnp.tanh(x)).astype(jnp.bfloat16)
        depth[...] = start3[...]
        top = jnp.zeros((8, wide), jnp.float32)
        for g in range(0, gpt, 8):
            top = top + jnp.exp2(-RATE * start3[pl.ds(g, 8), :])

        def one_level(k, above):
            part = pl.ds(pl.multiple_of(k * hid, hid), hid)
            raw = jnp.dot(w3t[...], second[part, :], preferred_element_type=jnp.float32)
            total = jnp.zeros((8, wide), jnp.float32)
            for g in range(0, gpt, chunk):
                at = pl.ds(g, chunk)
                y = raw[g : g + chunk] * LOG2E + bias3[at, :]
                soft = jnp.maximum(y, jnp.log2(1.0 + jnp.exp2(jnp.minimum(y, 64.0))))
                here = depth[at, :] + soft
                depth[at, :] = here
                left = jnp.exp2(-RATE * here)
                for piece in range(0, chunk, 8):
                    total = total + left[piece : piece + 8]
            heat[b, pl.ds(k, 1), :] = jnp.sum(above - total, axis=0, keepdims=True)
            return total

        lax.fori_loop(0, lev, one_level, top, unroll=4)
        back(b).start()
        return carry

    lax.fori_loop(0, blocks, absorb, 0)

    def placed(warm, at):
        high = warm.astype(jnp.bfloat16)
        rest = warm - high.astype(jnp.float32)
        mid = rest.astype(jnp.bfloat16)
        low = (rest - mid.astype(jnp.float32)).astype(jnp.bfloat16)
        out = lax.dot_general(
            jnp.concatenate([high, mid, low], axis=0),
            hot[:, pl.ds(at, half)],
            (((1,), (1,)), ((), ())),
            preferred_element_type=jnp.float32,
        )
        return out[:lev] + out[lev : 2 * lev] + out[2 * lev :]

    grid[...] = placed(jnp.concatenate([heat[b] for b in range(blocks)], axis=1), 0)
    for b in range(blocks):
        back(b).wait()
    grid[...] += placed(jnp.concatenate([heat_in[b] for b in range(blocks)], axis=1), half)
    for j in range(rows):
        warm = grid[:, j * lanes : (j + 1) * lanes]
        now_out[2, pl.ds(j, lev, stride=rows), :] = temper[j] + warm


def body(
    state_prev,
    state_now,
    stride_table,
    filter_len,
    zonal_coef,
    merid_coef,
    filter_coef,
    w_first,
    b_first,
    w_second,
    b_second,
    w_third,
    b_third,
    band_weight,
    sunlit_cols,
    sunlit_count,
):
    nvar, lev, rows, lanes = state_now.shape
    dims = (nvar, lev, rows, lanes, lax.axis_size("lon"), lax.axis_size("lat"))
    hid = w_second.shape[0]
    gpt = w_third.shape[1]
    flat = (nvar, lev * rows, lanes)
    half = sunlit_cols.size // 2
    wide = 2 * lanes
    blocks = half // wide
    vmem = pl.BlockSpec(memory_space=pltpu.VMEM)
    f32, bf16 = jnp.float32, jnp.bfloat16
    tile = (lev, lanes)
    shape = jax.ShapeDtypeStruct(flat, f32)
    operands = (
        state_prev.reshape(flat),
        state_now.reshape(flat),
        stride_table,
        filter_len,
        zonal_coef,
        sunlit_count,
        merid_coef[None],
        filter_coef[None],
        w_first,
        b_first[None],
        w_second,
        b_second[None],
        w_third,
        b_third[None],
        band_weight[None],
        sunlit_cols.reshape(1, -1),
    )
    spaces = [pltpu.VMEM] * 2 + [pltpu.SMEM] * 4 + [pltpu.VMEM] * 10
    prev, now = pl.pallas_call(
        functools.partial(kernel, dims, len(operands)),
        out_shape=(shape, shape),
        in_specs=[pl.BlockSpec(memory_space=pltpu.HBM)] * len(operands),
        out_specs=(vmem, vmem),
        scratch_shapes=[space(x.shape, x.dtype) for space, x in zip(spaces, operands)]
        + [
            pltpu.VMEM((nvar, rows + 2) + tile, f32),
            pltpu.VMEM((nvar, rows + 2) + tile, f32),
            pltpu.VMEM((nvar, rows) + tile, f32),
            pltpu.VMEM((rows,) + tile, f32),
            pltpu.VMEM((nvar * lev, rows * lanes), bf16),
            pltpu.VMEM((2, 2, nvar + 1) + tile, f32),
            pltpu.VMEM((2, 2, nvar + 1) + tile, f32),
            pltpu.VMEM((2, 2, nvar) + tile, f32),
            pltpu.VMEM((lev * hid, nvar * lev), bf16),
            pltpu.VMEM((hid, hid), bf16),
            pltpu.VMEM((gpt, hid), bf16),
            pltpu.VMEM((hid, wide), f32),
            pltpu.VMEM((hid, wide), f32),
            pltpu.VMEM((gpt, wide), f32),
            pltpu.VMEM((gpt, wide), f32),
            pltpu.VMEM((lev * hid, wide), bf16),
            pltpu.VMEM((lev * hid, wide), bf16),
            pltpu.VMEM((gpt, wide), f32),
            pltpu.VMEM((blocks, lev, wide), f32),
            pltpu.VMEM((rows * lanes, 2 * half), bf16),
            pltpu.VMEM((blocks, nvar * lev, wide), bf16),
            pltpu.VMEM((blocks, nvar * lev, wide), bf16),
            pltpu.VMEM((blocks, nvar * lev, wide), bf16),
            pltpu.VMEM((blocks, lev, wide), f32),
            pltpu.VMEM((lev, rows * lanes), f32),
            pltpu.SemaphoreType.DMA((len(operands),)),
            pltpu.SemaphoreType.DMA((2, 4)),
            pltpu.SemaphoreType.DMA((2, 4)),
            pltpu.SemaphoreType.DMA((2, blocks)),
            pltpu.SemaphoreType.DMA((2, blocks)),
        ],
        compiler_params=pltpu.CompilerParams(
            collective_id=0, has_side_effects=True, vmem_limit_bytes=63 * 1024 * 1024
        ),
    )(*operands)
    return prev.reshape(state_prev.shape), now.reshape(state_now.shape)


def solution(mesh):
    field = P(None, None, "lat", "lon")
    in_specs = (
        (field, field, P("lat"), P("lat"), P("lat"))
        + (P(),) * 9
        + (P("lat", "lon", None), P("lat", None))
    )
    return jax.shard_map(
        body, mesh=mesh, in_specs=in_specs, out_specs=(field, field), check_vma=False
    )
```

```python
import functools
import math

import jax
import jax.numpy as jnp
from jax import lax
from jax.experimental import pallas as pl
from jax.experimental.pallas import tpu as pltpu
from jax.sharding import PartitionSpec as P

SMAX = 32
POLAR = 4
MESH = pl.DeviceIdType.MESH
LOG2E = math.log2(math.e)
RATE = 0.15


def column(row, lanes):
    return jnp.transpose(jnp.broadcast_to(row, (lanes, row.shape[1])))


def flipped(weight):
    rows = weight.shape[0]
    eye = (
        lax.broadcasted_iota(jnp.int32, (rows, rows), 0)
        == lax.broadcasted_iota(jnp.int32, (rows, rows), 1)
    ).astype(jnp.float32).astype(jnp.bfloat16)
    return lax.dot_general(
        weight, eye, (((0,), (0,)), ((), ())), preferred_element_type=jnp.float32
    )


def kernel(dims, n_in, *refs):
    operands, refs = refs[:n_in], refs[n_in:]
    prev_hbm, now_hbm, refs = refs[0], refs[1], refs[2:]
    held, refs = refs[:n_in], refs[n_in:]
    (
        prev_ref,
        now_ref,
        stride_ref,
        flen_ref,
        zcoef_ref,
        count_ref,
        mcoef_ref,
        fcoef_ref,
        w1_ref,
        b1_ref,
        w2_ref,
        b2_ref,
        w3_ref,
        b3_ref,
        band_ref,
        list_ref,
    ) = held
    (
        prev_out,
        now_out,
        now0,
        now1,
        prev1,
        temper,
        feats,
        lon_out,
        lon_in,
        lat_in,
        w1big,
        w2t,
        w3t,
        bias1,
        bias2,
        bias3,
        start3,
        first,
        second,
        depth,
        heat,
        hot,
        own,
        gone,
        come,
        heat_in,
        grid,
        load_sem,
        save_sem,
        send_sem,
        recv_sem,
        far_send,
        far_recv,
    ) = refs
    nvar, lev, rows, lanes, n_lon, n_lat = dims
    hid = w2_ref.shape[0]
    gpt = w3_ref.shape[1]
    lon = lax.axis_index("lon")
    lat = lax.axis_index("lat")
    east = lax.rem(lon + 1, n_lon)
    west = lax.rem(lon + n_lon - 1, n_lon)
    far = lax.rem(lon + n_lon // 2, n_lon)
    at_top = lat == 0
    at_end = lat == n_lat - 1
    polar = jnp.logical_or(at_top, at_end)
    pstart = jnp.where(at_top, 0, rows - POLAR)
    body_lo = jnp.where(at_top, 1, 0)
    body_hi = jnp.where(at_end, rows // POLAR - 1, rows // POLAR)
    per = lanes // 2 // rows
    tiles = -(-nvar // per)

    loads = [
        pltpu.make_async_copy(src, dst, load_sem.at[i])
        for i, (src, dst) in enumerate(zip(operands, held))
    ]
    for i in (1, *range(2, n_in), 0):
        loads[i].start()

    barrier = pltpu.get_barrier_semaphore()
    for peer in (east, west, far):
        pl.semaphore_signal(barrier, inc=1, device_id={"lon": peer}, device_id_type=MESH)

    @pl.when(lat > 0)
    def _():
        pl.semaphore_signal(barrier, inc=1, device_id={"lat": lat - 1}, device_id_type=MESH)

    @pl.when(lat < n_lat - 1)
    def _():
        pl.semaphore_signal(barrier, inc=1, device_id={"lat": lat + 1}, device_id_type=MESH)

    lane = lax.broadcasted_iota(jnp.int32, (lev, lanes), 1)

    def zonal(turn, side, whole):
        part = pl.ds(0, nvar + tiles) if whole else pl.ds(nvar, tiles)
        return pltpu.make_async_remote_copy(
            src_ref=lon_out.at[turn, side, part],
            dst_ref=lon_in.at[turn, side, part],
            send_sem=send_sem.at[turn, side],
            recv_sem=recv_sem.at[turn, side],
            device_id={"lon": west if side == 0 else east},
            device_id_type=MESH,
        )

    def merid_copy(turn, side, src):
        return pltpu.make_async_remote_copy(
            src_ref=src.at[:, 1 if side == 0 else rows],
            dst_ref=lat_in.at[turn, side],
            send_sem=send_sem.at[turn, 2 + side],
            recv_sem=recv_sem.at[turn, 2 + side],
            device_id={"lat": lat - 1 if side == 0 else lat + 1},
            device_id_type=MESH,
        )

    def send_rows(turn, src):
        @pl.when(lat > 0)
        def _():
            merid_copy(turn, 0, src).start()

        @pl.when(lat < n_lat - 1)
        def _():
            merid_copy(turn, 1, src).start()

    def packed(edges, v, j, x):
        t, place = v // per, (v % per) * rows + j
        turned = pltpu.roll(x, lax.rem(2 * place + 1, lanes), 1)
        edges = list(edges)
        edges[t] = jnp.where(lane // 2 == place, turned, edges[t])
        return tuple(edges)

    no_edges = (jnp.zeros((lev, lanes), jnp.float32),) * tiles

    def send_sides(turn, src, edges):
        for t in range(tiles):
            lon_out[turn, 0, nvar + t] = edges[t]
            lon_out[turn, 1, nvar + t] = edges[t]

        @pl.when(polar)
        def _():
            for v in range(nvar):
                head = jnp.zeros((lev, lanes), jnp.float32)
                tail = head
                for q in range(POLAR):
                    x = src[v, pstart + q + 1]
                    turned = pltpu.roll(x, SMAX * q, 1) if q else x
                    head = jnp.where(lane // SMAX == q, turned, head)
                    tail = jnp.where(lane // SMAX == (q + POLAR - 1) % POLAR, turned, tail)
                lon_out[turn, 0, v] = head
                lon_out[turn, 1, v] = tail
            zonal(turn, 0, True).start()
            zonal(turn, 1, True).start()

        @pl.when(jnp.logical_not(polar))
        def _():
            zonal(turn, 0, False).start()
            zonal(turn, 1, False).start()

    def finish(turn, src):
        @pl.when(polar)
        def _():
            zonal(turn, 0, True).wait()
            zonal(turn, 1, True).wait()

        @pl.when(jnp.logical_not(polar))
        def _():
            zonal(turn, 0, False).wait()
            zonal(turn, 1, False).wait()

        @pl.when(lat > 0)
        def _():
            merid_copy(turn, 0, src).wait_send()
            merid_copy(turn, 1, src).wait_recv()
            for v in range(nvar):
                src[v, 0] = lat_in[turn, 1, v]

        @pl.when(lat < n_lat - 1)
        def _():
            merid_copy(turn, 1, src).wait_send()
            merid_copy(turn, 0, src).wait_recv()
            for v in range(nvar):
                src[v, rows + 1] = lat_in[turn, 0, v]

        zero = jnp.zeros((lev, lanes), jnp.float32)

        @pl.when(at_top)
        def _():
            for v in range(nvar):
                src[v, 0] = zero

        @pl.when(at_end)
        def _():
            for v in range(nvar):
                src[v, rows + 1] = zero

    def leap(turn, src, get_prev, put):
        mcoef = column(mcoef_ref[...], lanes)
        fcoef = column(fcoef_ref[...], lanes)
        from_east = lon_in.at[turn, 0]
        from_west = lon_in.at[turn, 1]

        def emit(v, j, x, diff, ends, zu, mv):
            tend = zu * diff - mv * (src[v, j + 2] - src[v, j])
            tend = tend + fcoef * (ends - 2.0 * x)
            old = get_prev(v, j)
            new = old + tend
            put(v, j, x + 0.1 * (old - 2.0 * x + new), new)
            return new

        halos = [
            jnp.where(
                lane % 2 == 0,
                pltpu.roll(from_east[nvar + t], lanes - 1, 1),
                pltpu.roll(from_west[nvar + t], 1, 1),
            )
            for t in range(tiles)
        ]

        def plain(group, edges):
            for r in range(POLAR):
                j = group * POLAR + r
                zu = -zcoef_ref[j] * src[0, j + 1]
                mv = mcoef * src[1, j + 1]
                for v in range(nvar):
                    x = src[v, j + 1]
                    place = (v % per) * rows + j
                    side = pltpu.roll(halos[v // per], lanes - 1 - 2 * place, 1)
                    plus = jnp.where(lane == lanes - 1, side, pltpu.roll(x, lanes - 1, 1))
                    minus = jnp.where(lane == 0, side, pltpu.roll(x, 1, 1))
                    new = emit(v, j, x, plus - minus, plus + minus, zu, mv)
                    if turn == 0:
                        edges = packed(edges, v, j, new)
            return edges

        edges = lax.fori_loop(body_lo, body_hi, plain, no_edges if turn == 0 else ())

        @pl.when(polar)
        def _():
            for q in range(POLAR):
                j = pstart + q
                s = stride_ref[j]
                m = flen_ref[j]
                inv = 1.0 / jnp.full((lev, lanes), s, jnp.int32).astype(jnp.float32)
                zu = -zcoef_ref[j] * src[0, j + 1]
                mv = mcoef * src[1, j + 1]
                for v in range(nvar):
                    x = src[v, j + 1]
                    side = jnp.where(lane // SMAX == q, from_east[v], from_west[v])
                    if q:
                        side = pltpu.roll(side, lanes - SMAX * q, 1)
                    pair = []
                    for n in (s, m):
                        plus = pltpu.roll(jnp.where(lane < n, side, x), lanes - n, 1)
                        minus = pltpu.roll(jnp.where(lane >= lanes - n, side, x), n, 1)
                        pair.append((plus, minus))
                    diff = (pair[0][0] - pair[0][1]) * inv
                    emit(v, j, x, diff, pair[1][0] + pair[1][1], zu, mv)

        return edges

    def load(group, edges):
        for r in range(POLAR):
            j = group * POLAR + r
            for v in range(nvar):
                x = now_ref[v, pl.ds(j, lev, stride=rows), :]
                now0[v, j + 1] = x
                edges = packed(edges, v, j, x)
        return edges

    loads[1].wait()
    edges = lax.fori_loop(0, rows // POLAR, load, no_edges)
    pl.semaphore_wait(
        barrier, 3 + jnp.where(lat > 0, 1, 0) + jnp.where(lat < n_lat - 1, 1, 0)
    )

    send_rows(0, now0)
    send_sides(0, now0, edges)

    for i in (*range(2, n_in), 0):
        loads[i].wait()

    expand = (
        lax.broadcasted_iota(jnp.int32, (nvar, nvar * lev), 1) // lev
        == lax.broadcasted_iota(jnp.int32, (nvar, nvar * lev), 0)
    ).astype(jnp.float32).astype(jnp.bfloat16)
    spread = lax.dot_general(
        w1_ref[...], expand, (((0,), (0,)), ((), ())), preferred_element_type=jnp.float32
    )
    level = lax.broadcasted_iota(jnp.int32, (hid, nvar * lev), 1) % lev
    for k in range(lev):
        w1big[pl.ds(k * hid, hid), :] = jnp.where(level == k, spread, 0.0).astype(jnp.bfloat16)
    w2t[...] = flipped(w2_ref[...]).astype(jnp.bfloat16)
    w3t[...] = flipped(w3_ref[...]).astype(jnp.bfloat16)
    bias1[...] = column(0.5 * b1_ref[...], 2 * lanes)
    bias2[...] = column(0.5 * b2_ref[...], 2 * lanes)
    bias3[...] = column(LOG2E * b3_ref[...], 2 * lanes)
    start3[...] = column(jnp.log2(band_ref[...]) * (-1.0 / RATE), 2 * lanes)
    finish(0, now0)

    def put_first(v, j, filtered, new):
        prev1[v, j] = filtered
        now1[v, j + 1] = new

    edges = leap(0, now0, lambda v, j: prev_ref[v, pl.ds(j, lev, stride=rows), :], put_first)
    send_rows(1, now1)
    send_sides(1, now1, edges)

    half = list_ref.shape[1] // 2
    mine = count_ref[0, lon]
    other = count_ref[0, far]
    slot = lax.broadcasted_iota(jnp.int32, (8, half), 1)
    shift = jnp.minimum(other, half - 1)
    moved = pltpu.roll(jnp.broadcast_to(list_ref[:, half:], (8, half)), shift, 1)
    for side, (cols, live) in enumerate(
        (
            (jnp.broadcast_to(list_ref[:, :half], (8, half)), slot < mine),
            (moved, jnp.logical_and(slot >= other, slot < other + mine - half)),
        )
    ):
        cols = jnp.where(live, cols, -1)[:1]
        at = pl.ds(side * half, half)
        lane_hot = (
            lax.broadcasted_iota(jnp.int32, (lanes, half), 0) == cols % lanes
        ).astype(jnp.float32).astype(jnp.bfloat16)
        for j in range(rows):
            row_hot = (cols // lanes == j).astype(jnp.float32).astype(jnp.bfloat16)
            hot[pl.ds(j * lanes, lanes), at] = lane_hot * row_hot

    finish(1, now1)

    def put_second(v, j, filtered, new):
        prev_out[v, pl.ds(j, lev, stride=rows), :] = filtered
        at = pl.ds(pl.multiple_of(j * lanes, lanes), lanes)
        feats[pl.ds(v * lev, lev), at] = new.astype(jnp.bfloat16)
        if v == 2:
            temper[j] = new
        else:
            now_out[v, pl.ds(j, lev, stride=rows), :] = new

    leap(1, now1, lambda v, j: prev1[v, j], put_second)

    saves = [pltpu.make_async_copy(prev_out, prev_hbm, save_sem.at[0])]
    for i, (a, b) in enumerate(((0, 2), (3, nvar), (2, 3))):
        part = pl.ds(a, b - a)
        saves.append(pltpu.make_async_copy(now_out.at[part], now_hbm.at[part], save_sem.at[i + 1]))
    for save in saves[:3]:
        save.start()

    wide = 2 * lanes
    chunk = 16
    blocks = half // wide

    def picked(at):
        got = jnp.dot(feats[...], hot[:, pl.ds(at, wide)], preferred_element_type=jnp.float32)
        return got.astype(jnp.bfloat16)

    def to_far(b):
        return pltpu.make_async_remote_copy(
            src_ref=gone.at[b],
            dst_ref=come.at[b],
            send_sem=far_send.at[0, b],
            recv_sem=far_recv.at[0, b],
            device_id={"lon": far},
            device_id_type=MESH,
        )

    def back(b):
        return pltpu.make_async_remote_copy(
            src_ref=heat.at[b],
            dst_ref=heat_in.at[b],
            send_sem=far_send.at[1, b],
            recv_sem=far_recv.at[1, b],
            device_id={"lon": far},
            device_id_type=MESH,
        )

    for b in range(blocks):
        gone[b] = picked(half + b * wide)
        to_far(b).start()
    for b in range(blocks):
        own[b] = picked(b * wide)

    def absorb(b, carry):
        to_far(b).wait()
        cells = own[b] + come[b]
        for k in range(lev):
            part = pl.ds(k * hid, hid)
            x = 0.5 * jnp.dot(w1big[part, :], cells, preferred_element_type=jnp.float32) + bias1[...]
            first[part, :] = (x + x * jnp.tanh(x)).astype(jnp.bfloat16)
        for k in range(lev):
            part = pl.ds(k * hid, hid)
            x = 0.5 * jnp.dot(w2t[...], first[part, :], preferred_element_type=jnp.float32) + bias2[...]
            second[part, :] = (x + x * jnp.tanh(x)).astype(jnp.bfloat16)
        depth[...] = start3[...]
        top = jnp.zeros((8, wide), jnp.float32)
        for g in range(0, gpt, 8):
            top = top + jnp.exp2(-RATE * start3[pl.ds(g, 8), :])

        def one_level(k, above):
            part = pl.ds(pl.multiple_of(k * hid, hid), hid)
            raw = jnp.dot(w3t[...], second[part, :], preferred_element_type=jnp.float32)
            total = jnp.zeros((8, wide), jnp.float32)
            for g in range(0, gpt, chunk):
                at = pl.ds(g, chunk)
                y = raw[g : g + chunk] * LOG2E + bias3[at, :]
                soft = jnp.maximum(y, jnp.log2(1.0 + jnp.exp2(jnp.minimum(y, 64.0))))
                here = depth[at, :] + soft
                depth[at, :] = here
                left = jnp.exp2(-RATE * here)
                for piece in range(0, chunk, 8):
                    total = total + left[piece : piece + 8]
            heat[b, pl.ds(k, 1), :] = jnp.sum(above - total, axis=0, keepdims=True)
            return total

        lax.fori_loop(0, lev, one_level, top, unroll=8)
        back(b).start()
        return carry

    lax.fori_loop(0, blocks, absorb, 0)

    def placed(warm, at):
        high = warm.astype(jnp.bfloat16)
        rest = warm - high.astype(jnp.float32)
        mid = rest.astype(jnp.bfloat16)
        low = (rest - mid.astype(jnp.float32)).astype(jnp.bfloat16)
        out = lax.dot_general(
            jnp.concatenate([high, mid, low], axis=0),
            hot[:, pl.ds(at, half)],
            (((1,), (1,)), ((), ())),
            preferred_element_type=jnp.float32,
        )
        return out[:lev] + out[lev : 2 * lev] + out[2 * lev :]

    grid[...] = placed(jnp.concatenate([heat[b] for b in range(blocks)], axis=1), 0)
    for b in range(blocks):
        back(b).wait()
    grid[...] += placed(jnp.concatenate([heat_in[b] for b in range(blocks)], axis=1), half)
    for j in range(rows):
        warm = grid[:, j * lanes : (j + 1) * lanes]
        now_out[2, pl.ds(j, lev, stride=rows), :] = temper[j] + warm
    saves[3].start()
    for save in saves:
        save.wait()


def hand_on(prev_ref, now_ref, prev_out, now_out, sem):
    copies = []
    for i, (src, dst) in enumerate(((prev_ref, prev_out), (now_ref, now_out))):
        for v in range(src.shape[0]):
            copies.append(pltpu.make_async_copy(src.at[v], dst.at[v], sem.at[i, v]))
    for copy in copies:
        copy.start()
    for copy in copies:
        copy.wait()


def body(
    state_prev,
    state_now,
    stride_table,
    filter_len,
    zonal_coef,
    merid_coef,
    filter_coef,
    w_first,
    b_first,
    w_second,
    b_second,
    w_third,
    b_third,
    band_weight,
    sunlit_cols,
    sunlit_count,
):
    nvar, lev, rows, lanes = state_now.shape
    dims = (nvar, lev, rows, lanes, lax.axis_size("lon"), lax.axis_size("lat"))
    hid = w_second.shape[0]
    gpt = w_third.shape[1]
    flat = (nvar, lev * rows, lanes)
    half = sunlit_cols.size // 2
    wide = 2 * lanes
    blocks = half // wide
    tiles = -(-nvar // (lanes // 2 // rows))
    hbm = pl.BlockSpec(memory_space=pltpu.HBM)
    limit = 63 * 1024 * 1024
    f32, bf16 = jnp.float32, jnp.bfloat16
    tile = (lev, lanes)
    shape = jax.ShapeDtypeStruct(flat, f32)
    operands = (
        state_prev.reshape(flat),
        state_now.reshape(flat),
        stride_table,
        filter_len,
        zonal_coef,
        sunlit_count,
        merid_coef[None],
        filter_coef[None],
        w_first,
        b_first[None],
        w_second,
        b_second[None],
        w_third,
        b_third[None],
        band_weight[None],
        sunlit_cols.reshape(1, -1),
    )
    spaces = [pltpu.VMEM] * 2 + [pltpu.SMEM] * 4 + [pltpu.VMEM] * 10
    prev, now = pl.pallas_call(
        functools.partial(kernel, dims, len(operands)),
        out_shape=(shape, shape),
        in_specs=[hbm] * len(operands),
        out_specs=(hbm, hbm),
        scratch_shapes=[space(x.shape, x.dtype) for space, x in zip(spaces, operands)]
        + [
            pltpu.VMEM(flat, f32),
            pltpu.VMEM(flat, f32),
            pltpu.VMEM((nvar, rows + 2) + tile, f32),
            pltpu.VMEM((nvar, rows + 2) + tile, f32),
            pltpu.VMEM((nvar, rows) + tile, f32),
            pltpu.VMEM((rows,) + tile, f32),
            pltpu.VMEM((nvar * lev, rows * lanes), bf16),
            pltpu.VMEM((2, 2, nvar + tiles) + tile, f32),
            pltpu.VMEM((2, 2, nvar + tiles) + tile, f32),
            pltpu.VMEM((2, 2, nvar) + tile, f32),
            pltpu.VMEM((lev * hid, nvar * lev), bf16),
            pltpu.VMEM((hid, hid), bf16),
            pltpu.VMEM((gpt, hid), bf16),
            pltpu.VMEM((hid, wide), f32),
            pltpu.VMEM((hid, wide), f32),
            pltpu.VMEM((gpt, wide), f32),
            pltpu.VMEM((gpt, wide), f32),
            pltpu.VMEM((lev * hid, wide), bf16),
            pltpu.VMEM((lev * hid, wide), bf16),
            pltpu.VMEM((gpt, wide), f32),
            pltpu.VMEM((blocks, lev, wide), f32),
            pltpu.VMEM((rows * lanes, 2 * half), bf16),
            pltpu.VMEM((blocks, nvar * lev, wide), bf16),
            pltpu.VMEM((blocks, nvar * lev, wide), bf16),
            pltpu.VMEM((blocks, nvar * lev, wide), bf16),
            pltpu.VMEM((blocks, lev, wide), f32),
            pltpu.VMEM((lev, rows * lanes), f32),
            pltpu.SemaphoreType.DMA((len(operands),)),
            pltpu.SemaphoreType.DMA((4,)),
            pltpu.SemaphoreType.DMA((2, 4)),
            pltpu.SemaphoreType.DMA((2, 4)),
            pltpu.SemaphoreType.DMA((2, blocks)),
            pltpu.SemaphoreType.DMA((2, blocks)),
        ],
        compiler_params=pltpu.CompilerParams(
            collective_id=0, has_side_effects=True, vmem_limit_bytes=limit
        ),
    )(*operands)
    prev, now = pl.pallas_call(
        hand_on,
        out_shape=(shape, shape),
        in_specs=[hbm, hbm],
        out_specs=(hbm, hbm),
        scratch_shapes=[pltpu.SemaphoreType.DMA((2, nvar))],
        compiler_params=pltpu.CompilerParams(vmem_limit_bytes=limit),
    )(prev, now)
    return prev.reshape(state_prev.shape), now.reshape(state_now.shape)


def solution(mesh):
    field = P(None, None, "lat", "lon")
    in_specs = (
        (field, field, P("lat"), P("lat"), P("lat"))
        + (P(),) * 9
        + (P("lat", "lon", None), P("lat", None))
    )
    return jax.shard_map(
        body, mesh=mesh, in_specs=in_specs, out_specs=(field, field), check_vma=False
    )
```

```python
import functools
import math

import jax
import jax.numpy as jnp
from jax import lax
from jax.experimental import pallas as pl
from jax.experimental.pallas import tpu as pltpu
from jax.sharding import PartitionSpec as P

SMAX = 32
POLAR = 4
MESH = pl.DeviceIdType.MESH
LOG2E = math.log2(math.e)
RATE = 0.15


def column(row, lanes):
    return jnp.transpose(jnp.broadcast_to(row, (lanes, row.shape[1])))


def flipped(weight):
    rows = weight.shape[0]
    eye = (
        lax.broadcasted_iota(jnp.int32, (rows, rows), 0)
        == lax.broadcasted_iota(jnp.int32, (rows, rows), 1)
    ).astype(jnp.float32).astype(jnp.bfloat16)
    return lax.dot_general(
        weight, eye, (((0,), (0,)), ((), ())), preferred_element_type=jnp.float32
    )


def kernel(dims, n_in, *refs):
    operands, refs = refs[:n_in], refs[n_in:]
    prev_hbm, now_hbm, refs = refs[0], refs[1], refs[2:]
    held, refs = refs[:n_in], refs[n_in:]
    (
        prev_ref,
        now_ref,
        stride_ref,
        flen_ref,
        zcoef_ref,
        count_ref,
        mcoef_ref,
        fcoef_ref,
        w1_ref,
        b1_ref,
        w2_ref,
        b2_ref,
        w3_ref,
        b3_ref,
        band_ref,
        list_ref,
    ) = held
    (
        prev_out,
        now_out,
        now0,
        now1,
        prev1,
        temper,
        feats,
        lon_out,
        lon_in,
        lat_in,
        w1big,
        w2t,
        w3t,
        bias1,
        bias2,
        bias3,
        start3,
        first,
        second,
        depth,
        heat,
        hot,
        own,
        gone,
        come,
        heat_in,
        grid,
        load_sem,
        save_sem,
        send_sem,
        recv_sem,
        far_send,
        far_recv,
    ) = refs
    nvar, lev, rows, lanes, n_lon, n_lat = dims
    hid = w2_ref.shape[0]
    gpt = w3_ref.shape[1]
    lon = lax.axis_index("lon")
    lat = lax.axis_index("lat")
    east = lax.rem(lon + 1, n_lon)
    west = lax.rem(lon + n_lon - 1, n_lon)
    far = lax.rem(lon + n_lon // 2, n_lon)
    at_top = lat == 0
    at_end = lat == n_lat - 1
    polar = jnp.logical_or(at_top, at_end)
    pstart = jnp.where(at_top, 0, rows - POLAR)
    per = lanes // 2 // rows
    tiles = -(-nvar // per)

    loads = [
        pltpu.make_async_copy(src, dst, load_sem.at[i])
        for i, (src, dst) in enumerate(zip(operands, held))
    ]
    for i in (1, *range(2, n_in), 0):
        loads[i].start()

    barrier = pltpu.get_barrier_semaphore()
    for peer in (east, west, far):
        pl.semaphore_signal(barrier, inc=1, device_id={"lon": peer}, device_id_type=MESH)

    @pl.when(lat > 0)
    def _():
        pl.semaphore_signal(barrier, inc=1, device_id={"lat": lat - 1}, device_id_type=MESH)

    @pl.when(lat < n_lat - 1)
    def _():
        pl.semaphore_signal(barrier, inc=1, device_id={"lat": lat + 1}, device_id_type=MESH)

    lane = lax.broadcasted_iota(jnp.int32, (lev, lanes), 1)

    def zonal(turn, side, kind):
        part = pl.ds(nvar, tiles) if kind else pl.ds(0, nvar)
        return pltpu.make_async_remote_copy(
            src_ref=lon_out.at[turn, side, part],
            dst_ref=lon_in.at[turn, side, part],
            send_sem=send_sem.at[turn, 2 * kind + side],
            recv_sem=recv_sem.at[turn, 2 * kind + side],
            device_id={"lon": west if side == 0 else east},
            device_id_type=MESH,
        )

    def merid_copy(turn, side, src):
        return pltpu.make_async_remote_copy(
            src_ref=src.at[:, 1 if side == 0 else rows],
            dst_ref=lat_in.at[turn, side],
            send_sem=send_sem.at[turn, 4 + side],
            recv_sem=recv_sem.at[turn, 4 + side],
            device_id={"lat": lat - 1 if side == 0 else lat + 1},
            device_id_type=MESH,
        )

    def send_rows(turn, src):
        @pl.when(lat > 0)
        def _():
            merid_copy(turn, 0, src).start()

        @pl.when(lat < n_lat - 1)
        def _():
            merid_copy(turn, 1, src).start()

    def packed(edges, v, j, x):
        t, place = v // per, (v % per) * rows + j
        turned = pltpu.roll(x, lax.rem(2 * place + 1, lanes), 1)
        edges = list(edges)
        edges[t] = jnp.where(lane // 2 == place, turned, edges[t])
        return tuple(edges)

    no_edges = (jnp.zeros((lev, lanes), jnp.float32),) * tiles

    def send_polar(turn, src):
        for v in range(nvar):
            head = jnp.zeros((lev, lanes), jnp.float32)
            tail = head
            for q in range(POLAR):
                x = src[v, pstart + q + 1]
                turned = pltpu.roll(x, SMAX * q, 1) if q else x
                head = jnp.where(lane // SMAX == q, turned, head)
                tail = jnp.where(lane // SMAX == (q + POLAR - 1) % POLAR, turned, tail)
            lon_out[turn, 0, v] = head
            lon_out[turn, 1, v] = tail
        zonal(turn, 0, 0).start()
        zonal(turn, 1, 0).start()

    def send_early(turn, src):
        send_rows(turn, src)

        @pl.when(polar)
        def _():
            send_polar(turn, src)

    def send_edges(turn):
        for t in range(tiles):
            lon_out[turn, 1, nvar + t] = lon_out[turn, 0, nvar + t]
        zonal(turn, 0, 1).start()
        zonal(turn, 1, 1).start()

    groups = rows // POLAR

    def group_at(i):
        return jnp.where(i == 0, 0, jnp.where(i == 1, groups - 1, i - 1))

    def held_edges(turn):
        return tuple(lon_out[turn, 0, nvar + t] for t in range(tiles))

    def hold_edges(turn, edges):
        for t in range(tiles):
            lon_out[turn, 0, nvar + t] = edges[t]

    def finish(turn, src):
        zonal(turn, 0, 1).wait()
        zonal(turn, 1, 1).wait()

        @pl.when(polar)
        def _():
            zonal(turn, 0, 0).wait()
            zonal(turn, 1, 0).wait()

        @pl.when(lat > 0)
        def _():
            merid_copy(turn, 0, src).wait_send()
            merid_copy(turn, 1, src).wait_recv()
            for v in range(nvar):
                src[v, 0] = lat_in[turn, 1, v]

        @pl.when(lat < n_lat - 1)
        def _():
            merid_copy(turn, 1, src).wait_send()
            merid_copy(turn, 0, src).wait_recv()
            for v in range(nvar):
                src[v, rows + 1] = lat_in[turn, 0, v]

        zero = jnp.zeros((lev, lanes), jnp.float32)

        @pl.when(at_top)
        def _():
            for v in range(nvar):
                src[v, 0] = zero

        @pl.when(at_end)
        def _():
            for v in range(nvar):
                src[v, rows + 1] = zero

    def leap(turn, src, get_prev, put):
        mcoef = column(mcoef_ref[...], lanes)
        fcoef = column(fcoef_ref[...], lanes)
        from_east = lon_in.at[turn, 0]
        from_west = lon_in.at[turn, 1]

        def emit(v, j, x, diff, ends, zu, mv):
            tend = zu * diff - mv * (src[v, j + 2] - src[v, j])
            tend = tend + fcoef * (ends - 2.0 * x)
            old = get_prev(v, j)
            new = old + tend
            put(v, j, x + 0.1 * (old - 2.0 * x + new), new)
            return new

        halos = [
            jnp.where(
                lane % 2 == 0,
                pltpu.roll(from_east[nvar + t], lanes - 1, 1),
                pltpu.roll(from_west[nvar + t], 1, 1),
            )
            for t in range(tiles)
        ]

        def plain(group):
            edges = held_edges(1) if turn == 0 else ()
            for r in range(POLAR):
                j = group * POLAR + r
                zu = -zcoef_ref[j] * src[0, j + 1]
                mv = mcoef * src[1, j + 1]
                for v in range(nvar):
                    x = src[v, j + 1]
                    place = (v % per) * rows + j
                    side = pltpu.roll(halos[v // per], lanes - 1 - 2 * place, 1)
                    plus = jnp.where(lane == lanes - 1, side, pltpu.roll(x, lanes - 1, 1))
                    minus = jnp.where(lane == 0, side, pltpu.roll(x, 1, 1))
                    new = emit(v, j, x, plus - minus, plus + minus, zu, mv)
                    if turn == 0:
                        edges = packed(edges, v, j, new)
            if turn == 0:
                hold_edges(1, edges)

        @pl.when(polar)
        def _():
            for q in range(POLAR):
                j = pstart + q
                s = stride_ref[j]
                m = flen_ref[j]
                inv = 1.0 / jnp.full((lev, lanes), s, jnp.int32).astype(jnp.float32)
                zu = -zcoef_ref[j] * src[0, j + 1]
                mv = mcoef * src[1, j + 1]
                for v in range(nvar):
                    x = src[v, j + 1]
                    side = jnp.where(lane // SMAX == q, from_east[v], from_west[v])
                    if q:
                        side = pltpu.roll(side, lanes - SMAX * q, 1)
                    pair = []
                    for n in (s, m):
                        plus = pltpu.roll(jnp.where(lane < n, side, x), lanes - n, 1)
                        minus = pltpu.roll(jnp.where(lane >= lanes - n, side, x), n, 1)
                        pair.append((plus, minus))
                    diff = (pair[0][0] - pair[0][1]) * inv
                    emit(v, j, x, diff, pair[1][0] + pair[1][1], zu, mv)

        def one_group(i, carry):
            group = group_at(i)
            skip = jnp.logical_or(
                jnp.logical_and(at_top, group == 0), jnp.logical_and(at_end, group == groups - 1)
            )

            @pl.when(jnp.logical_not(skip))
            def _():
                plain(group)

            if turn == 0:

                @pl.when(i == 1)
                def _():
                    send_early(1, now1)

            return carry

        if turn == 0:
            hold_edges(1, no_edges)
        lax.fori_loop(0, groups, one_group, 0)

    def load(i, carry):
        group = group_at(i)
        edges = held_edges(0)
        for r in range(POLAR):
            j = group * POLAR + r
            for v in range(nvar):
                x = now_ref[v, pl.ds(j, lev, stride=rows), :]
                now0[v, j + 1] = x
                edges = packed(edges, v, j, x)
        hold_edges(0, edges)

        @pl.when(i == 1)
        def _():
            send_early(0, now0)

        return carry

    hold_edges(0, no_edges)
    loads[1].wait()
    pl.semaphore_wait(
        barrier, 3 + jnp.where(lat > 0, 1, 0) + jnp.where(lat < n_lat - 1, 1, 0)
    )

    lax.fori_loop(0, groups, load, 0)
    send_edges(0)

    for i in (*range(2, n_in), 0):
        loads[i].wait()

    expand = (
        lax.broadcasted_iota(jnp.int32, (nvar, nvar * lev), 1) // lev
        == lax.broadcasted_iota(jnp.int32, (nvar, nvar * lev), 0)
    ).astype(jnp.float32).astype(jnp.bfloat16)
    spread = lax.dot_general(
        w1_ref[...], expand, (((0,), (0,)), ((), ())), preferred_element_type=jnp.float32
    )
    level = lax.broadcasted_iota(jnp.int32, (hid, nvar * lev), 1) % lev
    for k in range(lev):
        w1big[pl.ds(k * hid, hid), :] = jnp.where(level == k, 0.5 * spread, 0.0).astype(jnp.bfloat16)
    w2t[...] = (0.5 * flipped(w2_ref[...])).astype(jnp.bfloat16)
    w3t[...] = flipped(w3_ref[...]).astype(jnp.bfloat16)
    bias1[...] = column(0.5 * b1_ref[...], 2 * lanes)
    bias2[...] = column(0.5 * b2_ref[...], 2 * lanes)
    bias3[...] = column(LOG2E * b3_ref[...], 2 * lanes)
    start3[...] = column(jnp.log2(band_ref[...]) * (-1.0 / RATE), 2 * lanes)
    finish(0, now0)

    def put_first(v, j, filtered, new):
        prev1[v, j] = filtered
        now1[v, j + 1] = new

    leap(0, now0, lambda v, j: prev_ref[v, pl.ds(j, lev, stride=rows), :], put_first)
    send_edges(1)

    half = list_ref.shape[1] // 2
    mine = count_ref[0, lon]
    other = count_ref[0, far]
    slot = lax.broadcasted_iota(jnp.int32, (8, half), 1)
    shift = jnp.minimum(other, half - 1)
    moved = pltpu.roll(jnp.broadcast_to(list_ref[:, half:], (8, half)), shift, 1)
    for side, (cols, live) in enumerate(
        (
            (jnp.broadcast_to(list_ref[:, :half], (8, half)), slot < mine),
            (moved, jnp.logical_and(slot >= other, slot < other + mine - half)),
        )
    ):
        cols = jnp.where(live, cols, -1)[:1]
        at = pl.ds(side * half, half)
        lane_hot = (
            lax.broadcasted_iota(jnp.int32, (lanes, half), 0) == cols % lanes
        ).astype(jnp.float32).astype(jnp.bfloat16)
        for j in range(rows):
            row_hot = (cols // lanes == j).astype(jnp.float32).astype(jnp.bfloat16)
            hot[pl.ds(j * lanes, lanes), at] = lane_hot * row_hot

    finish(1, now1)

    def put_second(v, j, filtered, new):
        prev_out[v, pl.ds(j, lev, stride=rows), :] = filtered
        at = pl.ds(pl.multiple_of(j * lanes, lanes), lanes)
        feats[pl.ds(v * lev, lev), at] = new.astype(jnp.bfloat16)
        if v == 2:
            temper[j] = new
        else:
            now_out[v, pl.ds(j, lev, stride=rows), :] = new

    leap(1, now1, lambda v, j: prev1[v, j], put_second)

    saves = [pltpu.make_async_copy(prev_out, prev_hbm, save_sem.at[0])]
    for i, (a, b) in enumerate(((0, 2), (3, nvar), (2, 3))):
        part = pl.ds(a, b - a)
        saves.append(pltpu.make_async_copy(now_out.at[part], now_hbm.at[part], save_sem.at[i + 1]))
    for save in saves[:3]:
        save.start()

    wide = 2 * lanes
    chunk = 16
    blocks = half // wide

    def picked(at):
        got = jnp.dot(feats[...], hot[:, pl.ds(at, wide)], preferred_element_type=jnp.float32)
        return got.astype(jnp.bfloat16)

    def to_far(b):
        return pltpu.make_async_remote_copy(
            src_ref=gone.at[b],
            dst_ref=come.at[b],
            send_sem=far_send.at[0, b],
            recv_sem=far_recv.at[0, b],
            device_id={"lon": far},
            device_id_type=MESH,
        )

    def back(b):
        return pltpu.make_async_remote_copy(
            src_ref=heat.at[b],
            dst_ref=heat_in.at[b],
            send_sem=far_send.at[1, b],
            recv_sem=far_recv.at[1, b],
            device_id={"lon": far},
            device_id_type=MESH,
        )

    for b in range(blocks):
        gone[b] = picked(half + b * wide)
        to_far(b).start()
    for b in range(blocks):
        own[b] = picked(b * wide)

    def absorb(b, carry):
        to_far(b).wait()
        cells = own[b] + come[b]
        for k in range(lev):
            part = pl.ds(k * hid, hid)
            x = jnp.dot(w1big[part, :], cells, preferred_element_type=jnp.float32) + bias1[...]
            first[part, :] = (x + x * jnp.tanh(x)).astype(jnp.bfloat16)
        for k in range(lev):
            part = pl.ds(k * hid, hid)
            x = jnp.dot(w2t[...], first[part, :], preferred_element_type=jnp.float32) + bias2[...]
            second[part, :] = (x + x * jnp.tanh(x)).astype(jnp.bfloat16)
        depth[...] = start3[...]
        top = jnp.zeros((8, wide), jnp.float32)
        for g in range(0, gpt, 8):
            top = top + jnp.exp2(-RATE * start3[pl.ds(g, 8), :])

        def one_level(k, above):
            part = pl.ds(k * hid, hid)
            raw = jnp.dot(w3t[...], second[part, :], preferred_element_type=jnp.float32)
            total = jnp.zeros((8, wide), jnp.float32)
            for g in range(0, gpt, chunk):
                at = pl.ds(g, chunk)
                y = raw[g : g + chunk] * LOG2E + bias3[at, :]
                soft = jnp.maximum(y, jnp.log2(1.0 + jnp.exp2(jnp.minimum(y, 64.0))))
                here = depth[at, :] + soft
                depth[at, :] = here
                left = jnp.exp2(-RATE * here)
                for piece in range(0, chunk, 8):
                    total = total + left[piece : piece + 8]
            heat[b, pl.ds(k, 1), :] = jnp.sum(above - total, axis=0, keepdims=True)
            return total

        above = top
        for k in range(lev):
            above = one_level(k, above)
        back(b).start()
        return carry

    lax.fori_loop(0, blocks, absorb, 0)

    def placed(warm, at):
        high = warm.astype(jnp.bfloat16)
        rest = warm - high.astype(jnp.float32)
        mid = rest.astype(jnp.bfloat16)
        low = (rest - mid.astype(jnp.float32)).astype(jnp.bfloat16)
        out = lax.dot_general(
            jnp.concatenate([high, mid, low], axis=0),
            hot[:, pl.ds(at, half)],
            (((1,), (1,)), ((), ())),
            preferred_element_type=jnp.float32,
        )
        return out[:lev] + out[lev : 2 * lev] + out[2 * lev :]

    grid[...] = placed(jnp.concatenate([heat[b] for b in range(blocks)], axis=1), 0)
    for b in range(blocks):
        back(b).wait()
    grid[...] += placed(jnp.concatenate([heat_in[b] for b in range(blocks)], axis=1), half)
    for j in range(rows):
        warm = grid[:, j * lanes : (j + 1) * lanes]
        now_out[2, pl.ds(j, lev, stride=rows), :] = temper[j] + warm
    saves[3].start()
    for save in saves:
        save.wait()


def hand_on(prev_ref, now_ref, prev_out, now_out, stage, sem):
    ins, outs = [], []
    for i, (src, dst) in enumerate(((prev_ref, prev_out), (now_ref, now_out))):
        for v in range(src.shape[0]):
            ins.append(pltpu.make_async_copy(src.at[v], stage.at[i, v], sem.at[0, i, v]))
            outs.append(pltpu.make_async_copy(stage.at[i, v], dst.at[v], sem.at[1, i, v]))
    for copy in ins:
        copy.start()
    for copy, out in zip(ins, outs):
        copy.wait()
        out.start()
    for out in outs:
        out.wait()


def body(
    state_prev,
    state_now,
    stride_table,
    filter_len,
    zonal_coef,
    merid_coef,
    filter_coef,
    w_first,
    b_first,
    w_second,
    b_second,
    w_third,
    b_third,
    band_weight,
    sunlit_cols,
    sunlit_count,
):
    nvar, lev, rows, lanes = state_now.shape
    dims = (nvar, lev, rows, lanes, lax.axis_size("lon"), lax.axis_size("lat"))
    hid = w_second.shape[0]
    gpt = w_third.shape[1]
    flat = (nvar, lev * rows, lanes)
    half = sunlit_cols.size // 2
    wide = 2 * lanes
    blocks = half // wide
    tiles = -(-nvar // (lanes // 2 // rows))
    hbm = pl.BlockSpec(memory_space=pltpu.HBM)
    limit = 63 * 1024 * 1024
    f32, bf16 = jnp.float32, jnp.bfloat16
    tile = (lev, lanes)
    shape = jax.ShapeDtypeStruct(flat, f32)
    operands = (
        state_prev.reshape(flat),
        state_now.reshape(flat),
        stride_table,
        filter_len,
        zonal_coef,
        sunlit_count,
        merid_coef[None],
        filter_coef[None],
        w_first,
        b_first[None],
        w_second,
        b_second[None],
        w_third,
        b_third[None],
        band_weight[None],
        sunlit_cols.reshape(1, -1),
    )
    spaces = [pltpu.VMEM] * 2 + [pltpu.SMEM] * 4 + [pltpu.VMEM] * 10
    prev, now = pl.pallas_call(
        functools.partial(kernel, dims, len(operands)),
        out_shape=(shape, shape),
        in_specs=[hbm] * len(operands),
        out_specs=(hbm, hbm),
        scratch_shapes=[space(x.shape, x.dtype) for space, x in zip(spaces, operands)]
        + [
            pltpu.VMEM(flat, f32),
            pltpu.VMEM(flat, f32),
            pltpu.VMEM((nvar, rows + 2) + tile, f32),
            pltpu.VMEM((nvar, rows + 2) + tile, f32),
            pltpu.VMEM((nvar, rows) + tile, f32),
            pltpu.VMEM((rows,) + tile, f32),
            pltpu.VMEM((nvar * lev, rows * lanes), bf16),
            pltpu.VMEM((2, 2, nvar + tiles) + tile, f32),
            pltpu.VMEM((2, 2, nvar + tiles) + tile, f32),
            pltpu.VMEM((2, 2, nvar) + tile, f32),
            pltpu.VMEM((lev * hid, nvar * lev), bf16),
            pltpu.VMEM((hid, hid), bf16),
            pltpu.VMEM((gpt, hid), bf16),
            pltpu.VMEM((hid, wide), f32),
            pltpu.VMEM((hid, wide), f32),
            pltpu.VMEM((gpt, wide), f32),
            pltpu.VMEM((gpt, wide), f32),
            pltpu.VMEM((lev * hid, wide), bf16),
            pltpu.VMEM((lev * hid, wide), bf16),
            pltpu.VMEM((gpt, wide), f32),
            pltpu.VMEM((blocks, lev, wide), f32),
            pltpu.VMEM((rows * lanes, 2 * half), bf16),
            pltpu.VMEM((blocks, nvar * lev, wide), bf16),
            pltpu.VMEM((blocks, nvar * lev, wide), bf16),
            pltpu.VMEM((blocks, nvar * lev, wide), bf16),
            pltpu.VMEM((blocks, lev, wide), f32),
            pltpu.VMEM((lev, rows * lanes), f32),
            pltpu.SemaphoreType.DMA((len(operands),)),
            pltpu.SemaphoreType.DMA((4,)),
            pltpu.SemaphoreType.DMA((2, 6)),
            pltpu.SemaphoreType.DMA((2, 6)),
            pltpu.SemaphoreType.DMA((2, blocks)),
            pltpu.SemaphoreType.DMA((2, blocks)),
        ],
        compiler_params=pltpu.CompilerParams(
            collective_id=0, has_side_effects=True, vmem_limit_bytes=limit
        ),
    )(*operands)
    prev, now = pl.pallas_call(
        hand_on,
        out_shape=(shape, shape),
        in_specs=[hbm, hbm],
        out_specs=(hbm, hbm),
        scratch_shapes=[pltpu.VMEM((2,) + flat, f32), pltpu.SemaphoreType.DMA((2, 2, nvar))],
        compiler_params=pltpu.CompilerParams(vmem_limit_bytes=limit),
    )(prev, now)
    return prev.reshape(state_prev.shape), now.reshape(state_now.shape)


def solution(mesh):
    field = P(None, None, "lat", "lon")
    in_specs = (
        (field, field, P("lat"), P("lat"), P("lat"))
        + (P(),) * 9
        + (P("lat", "lon", None), P("lat", None))
    )
    return jax.shard_map(
        body, mesh=mesh, in_specs=in_specs, out_specs=(field, field), check_vma=False
    )
```

```python
import functools
import math

import jax
import jax.numpy as jnp
from jax import lax
from jax.experimental import pallas as pl
from jax.experimental.pallas import tpu as pltpu
from jax.sharding import PartitionSpec as P

SMAX = 32
POLAR = 4
MESH = pl.DeviceIdType.MESH
LOG2E = math.log2(math.e)
RATE = 0.15
FALL = -RATE * LOG2E


def column(row, lanes):
    return jnp.transpose(jnp.broadcast_to(row, (lanes, row.shape[1])))


def flipped(weight):
    rows = weight.shape[0]
    eye = (
        lax.broadcasted_iota(jnp.int32, (rows, rows), 0)
        == lax.broadcasted_iota(jnp.int32, (rows, rows), 1)
    ).astype(jnp.float32).astype(jnp.bfloat16)
    return lax.dot_general(
        weight, eye, (((0,), (0,)), ((), ())), preferred_element_type=jnp.float32
    )


def kernel(dims, n_in, *refs):
    operands, refs = refs[:n_in], refs[n_in:]
    prev_hbm, now_hbm, refs = refs[0], refs[1], refs[2:]
    held, refs = refs[:n_in], refs[n_in:]
    (
        prev_ref,
        now_ref,
        stride_ref,
        flen_ref,
        zcoef_ref,
        count_ref,
        mcoef_ref,
        fcoef_ref,
        w1_ref,
        b1_ref,
        w2_ref,
        b2_ref,
        w3_ref,
        b3_ref,
        band_ref,
        list_ref,
    ) = held
    (
        prev_out,
        now_out,
        now0,
        now1,
        prev1,
        temper,
        feats,
        lon_out,
        lon_in,
        lat_in,
        w1big,
        w2t,
        w3t,
        bias1,
        bias2,
        bias3,
        start3,
        first,
        second,
        depth,
        heat,
        hot,
        own,
        gone,
        come,
        heat_in,
        grid,
        load_sem,
        save_sem,
        send_sem,
        recv_sem,
        far_send,
        far_recv,
    ) = refs
    nvar, lev, rows, lanes, n_lon, n_lat = dims
    hid = w2_ref.shape[0]
    gpt = w3_ref.shape[1]
    lon = lax.axis_index("lon")
    lat = lax.axis_index("lat")
    east = lax.rem(lon + 1, n_lon)
    west = lax.rem(lon + n_lon - 1, n_lon)
    far = lax.rem(lon + n_lon // 2, n_lon)
    at_top = lat == 0
    at_end = lat == n_lat - 1
    polar = jnp.logical_or(at_top, at_end)
    pstart = jnp.where(at_top, 0, rows - POLAR)
    per = lanes // 2 // rows
    tiles = -(-nvar // per)

    loads = [
        pltpu.make_async_copy(src, dst, load_sem.at[i])
        for i, (src, dst) in enumerate(zip(operands, held))
    ]
    for i in (1, *range(2, n_in), 0):
        loads[i].start()

    barrier = pltpu.get_barrier_semaphore()
    for peer in (east, west, far):
        pl.semaphore_signal(barrier, inc=1, device_id={"lon": peer}, device_id_type=MESH)

    @pl.when(lat > 0)
    def _():
        pl.semaphore_signal(barrier, inc=1, device_id={"lat": lat - 1}, device_id_type=MESH)

    @pl.when(lat < n_lat - 1)
    def _():
        pl.semaphore_signal(barrier, inc=1, device_id={"lat": lat + 1}, device_id_type=MESH)

    lane = lax.broadcasted_iota(jnp.int32, (lev, lanes), 1)

    def zonal(turn, side, kind):
        part = pl.ds(nvar, tiles) if kind else pl.ds(0, nvar)
        return pltpu.make_async_remote_copy(
            src_ref=lon_out.at[turn, side, part],
            dst_ref=lon_in.at[turn, side, part],
            send_sem=send_sem.at[turn, 2 * kind + side],
            recv_sem=recv_sem.at[turn, 2 * kind + side],
            device_id={"lon": west if side == 0 else east},
            device_id_type=MESH,
        )

    def merid_copy(turn, side, src):
        return pltpu.make_async_remote_copy(
            src_ref=src.at[:, 1 if side == 0 else rows],
            dst_ref=lat_in.at[turn, side],
            send_sem=send_sem.at[turn, 4 + side],
            recv_sem=recv_sem.at[turn, 4 + side],
            device_id={"lat": lat - 1 if side == 0 else lat + 1},
            device_id_type=MESH,
        )

    def send_rows(turn, src):
        @pl.when(lat > 0)
        def _():
            merid_copy(turn, 0, src).start()

        @pl.when(lat < n_lat - 1)
        def _():
            merid_copy(turn, 1, src).start()

    def packed(edges, v, j, x):
        t, place = v // per, (v % per) * rows + j
        turned = pltpu.roll(x, lax.rem(2 * place + 1, lanes), 1)
        edges = list(edges)
        edges[t] = jnp.where(lane // 2 == place, turned, edges[t])
        return tuple(edges)

    no_edges = (jnp.zeros((lev, lanes), jnp.float32),) * tiles

    def send_polar(turn, src):
        for v in range(nvar):
            head = jnp.zeros((lev, lanes), jnp.float32)
            tail = head
            for q in range(POLAR):
                x = src[v, pstart + q + 1]
                turned = pltpu.roll(x, SMAX * q, 1) if q else x
                head = jnp.where(lane // SMAX == q, turned, head)
                tail = jnp.where(lane // SMAX == (q + POLAR - 1) % POLAR, turned, tail)
            lon_out[turn, 0, v] = head
            lon_out[turn, 1, v] = tail
        zonal(turn, 0, 0).start()
        zonal(turn, 1, 0).start()

    def send_early(turn, src):
        send_rows(turn, src)

        @pl.when(polar)
        def _():
            send_polar(turn, src)

    def send_edges(turn):
        for t in range(tiles):
            lon_out[turn, 1, nvar + t] = lon_out[turn, 0, nvar + t]
        zonal(turn, 0, 1).start()
        zonal(turn, 1, 1).start()

    groups = rows // POLAR

    def group_at(i):
        return jnp.where(i == 0, 0, jnp.where(i == 1, groups - 1, i - 1))

    def held_edges(turn):
        return tuple(lon_out[turn, 0, nvar + t] for t in range(tiles))

    def hold_edges(turn, edges):
        for t in range(tiles):
            lon_out[turn, 0, nvar + t] = edges[t]

    def finish(turn, src):
        zonal(turn, 0, 1).wait()
        zonal(turn, 1, 1).wait()

        @pl.when(polar)
        def _():
            zonal(turn, 0, 0).wait()
            zonal(turn, 1, 0).wait()

        @pl.when(lat > 0)
        def _():
            merid_copy(turn, 0, src).wait_send()
            merid_copy(turn, 1, src).wait_recv()
            for v in range(nvar):
                src[v, 0] = lat_in[turn, 1, v]

        @pl.when(lat < n_lat - 1)
        def _():
            merid_copy(turn, 1, src).wait_send()
            merid_copy(turn, 0, src).wait_recv()
            for v in range(nvar):
                src[v, rows + 1] = lat_in[turn, 0, v]

        zero = jnp.zeros((lev, lanes), jnp.float32)

        @pl.when(at_top)
        def _():
            for v in range(nvar):
                src[v, 0] = zero

        @pl.when(at_end)
        def _():
            for v in range(nvar):
                src[v, rows + 1] = zero

    def leap(turn, src, get_prev, put):
        mcoef = column(mcoef_ref[...], lanes)
        fcoef = column(fcoef_ref[...], lanes)
        from_east = lon_in.at[turn, 0]
        from_west = lon_in.at[turn, 1]

        def emit(v, j, x, diff, ends, zu, mv):
            tend = zu * diff - mv * (src[v, j + 2] - src[v, j])
            tend = tend + fcoef * (ends - 2.0 * x)
            old = get_prev(v, j)
            new = old + tend
            put(v, j, x + 0.1 * (old - 2.0 * x + new), new)
            return new

        halos = [
            jnp.where(
                lane % 2 == 0,
                pltpu.roll(from_east[nvar + t], lanes - 1, 1),
                pltpu.roll(from_west[nvar + t], 1, 1),
            )
            for t in range(tiles)
        ]

        def plain(group):
            edges = held_edges(1) if turn == 0 else ()
            for r in range(POLAR):
                j = group * POLAR + r
                zu = -zcoef_ref[j] * src[0, j + 1]
                mv = mcoef * src[1, j + 1]
                for v in range(nvar):
                    x = src[v, j + 1]
                    place = (v % per) * rows + j
                    side = pltpu.roll(halos[v // per], lanes - 1 - 2 * place, 1)
                    plus = jnp.where(lane == lanes - 1, side, pltpu.roll(x, lanes - 1, 1))
                    minus = jnp.where(lane == 0, side, pltpu.roll(x, 1, 1))
                    new = emit(v, j, x, plus - minus, plus + minus, zu, mv)
                    if turn == 0:
                        edges = packed(edges, v, j, new)
            if turn == 0:
                hold_edges(1, edges)

        @pl.when(polar)
        def _():
            for q in range(POLAR):
                j = pstart + q
                s = stride_ref[j]
                m = flen_ref[j]
                inv = 1.0 / jnp.full((lev, lanes), s, jnp.int32).astype(jnp.float32)
                zu = -zcoef_ref[j] * src[0, j + 1]
                mv = mcoef * src[1, j + 1]
                for v in range(nvar):
                    x = src[v, j + 1]
                    side = jnp.where(lane // SMAX == q, from_east[v], from_west[v])
                    if q:
                        side = pltpu.roll(side, lanes - SMAX * q, 1)
                    pair = []
                    for n in (s, m):
                        plus = pltpu.roll(jnp.where(lane < n, side, x), lanes - n, 1)
                        minus = pltpu.roll(jnp.where(lane >= lanes - n, side, x), n, 1)
                        pair.append((plus, minus))
                    diff = (pair[0][0] - pair[0][1]) * inv
                    emit(v, j, x, diff, pair[1][0] + pair[1][1], zu, mv)

        def one_group(i, carry):
            group = group_at(i)
            skip = jnp.logical_or(
                jnp.logical_and(at_top, group == 0), jnp.logical_and(at_end, group == groups - 1)
            )

            @pl.when(jnp.logical_not(skip))
            def _():
                plain(group)

            if turn == 0:

                @pl.when(i == 1)
                def _():
                    send_early(1, now1)

            return carry

        if turn == 0:
            hold_edges(1, no_edges)
        lax.fori_loop(0, groups, one_group, 0)

    def load(i, carry):
        group = group_at(i)
        edges = held_edges(0)
        for r in range(POLAR):
            j = group * POLAR + r
            for v in range(nvar):
                x = now_ref[v, pl.ds(j, lev, stride=rows), :]
                now0[v, j + 1] = x
                edges = packed(edges, v, j, x)
        hold_edges(0, edges)

        @pl.when(i == 1)
        def _():
            send_early(0, now0)

        return carry

    hold_edges(0, no_edges)
    loads[1].wait()
    pl.semaphore_wait(
        barrier, 3 + jnp.where(lat > 0, 1, 0) + jnp.where(lat < n_lat - 1, 1, 0)
    )

    lax.fori_loop(0, groups, load, 0)
    send_edges(0)

    for i in (*range(2, n_in), 0):
        loads[i].wait()

    expand = (
        lax.broadcasted_iota(jnp.int32, (nvar, nvar * lev), 1) // lev
        == lax.broadcasted_iota(jnp.int32, (nvar, nvar * lev), 0)
    ).astype(jnp.float32).astype(jnp.bfloat16)
    spread = lax.dot_general(
        w1_ref[...], expand, (((0,), (0,)), ((), ())), preferred_element_type=jnp.float32
    )
    level = lax.broadcasted_iota(jnp.int32, (hid, nvar * lev), 1) % lev
    for k in range(lev):
        w1big[pl.ds(k * hid, hid), :] = jnp.where(level == k, 0.5 * spread, 0.0).astype(jnp.bfloat16)
    w2t[...] = (0.5 * flipped(w2_ref[...])).astype(jnp.bfloat16)
    w3t[...] = flipped(w3_ref[...]).astype(jnp.bfloat16)
    bias1[...] = column(0.5 * b1_ref[...], lanes)
    bias2[...] = column(0.5 * b2_ref[...], lanes)
    bias3[...] = column(b3_ref[...], lanes)
    start3[...] = column(jnp.log(band_ref[...]) * (-1.0 / RATE), lanes)

    finish(0, now0)

    def put_first(v, j, filtered, new):
        prev1[v, j] = filtered
        now1[v, j + 1] = new

    leap(0, now0, lambda v, j: prev_ref[v, pl.ds(j, lev, stride=rows), :], put_first)
    send_edges(1)

    half = list_ref.shape[1] // 2
    mine = count_ref[0, lon]
    other = count_ref[0, far]
    slot = lax.broadcasted_iota(jnp.int32, (8, half), 1)
    shift = jnp.minimum(other, half - 1)
    moved = pltpu.roll(jnp.broadcast_to(list_ref[:, half:], (8, half)), shift, 1)
    for side, (cols, live) in enumerate(
        (
            (jnp.broadcast_to(list_ref[:, :half], (8, half)), slot < mine),
            (moved, jnp.logical_and(slot >= other, slot < other + mine - half)),
        )
    ):
        cols = jnp.where(live, cols, -1)[:1]
        at = pl.ds(side * half, half)
        lane_hot = (
            lax.broadcasted_iota(jnp.int32, (lanes, half), 0) == cols % lanes
        ).astype(jnp.float32).astype(jnp.bfloat16)
        for j in range(rows):
            row_hot = (cols // lanes == j).astype(jnp.float32).astype(jnp.bfloat16)
            hot[pl.ds(j * lanes, lanes), at] = lane_hot * row_hot

    finish(1, now1)

    def put_second(v, j, filtered, new):
        prev_out[v, pl.ds(j, lev, stride=rows), :] = filtered
        at = pl.ds(pl.multiple_of(j * lanes, lanes), lanes)
        feats[pl.ds(v * lev, lev), at] = new.astype(jnp.bfloat16)
        if v == 2:
            temper[j] = new
        else:
            now_out[v, pl.ds(j, lev, stride=rows), :] = new

    leap(1, now1, lambda v, j: prev1[v, j], put_second)

    saves = [pltpu.make_async_copy(prev_out, prev_hbm, save_sem.at[0])]
    for i, (a, b) in enumerate(((0, 2), (3, nvar), (2, 3))):
        part = pl.ds(a, b - a)
        saves.append(pltpu.make_async_copy(now_out.at[part], now_hbm.at[part], save_sem.at[i + 1]))
    for save in saves[:3]:
        save.start()

    wide = 2 * lanes
    chunk = 16
    blocks = half // wide
    merge = math.gcd(lev, 4)

    def doubled(x):
        return jnp.concatenate([x, x], axis=1)

    def picked(at):
        got = jnp.dot(feats[...], hot[:, pl.ds(at, wide)], preferred_element_type=jnp.float32)
        return got.astype(jnp.bfloat16)

    def to_far(b):
        return pltpu.make_async_remote_copy(
            src_ref=gone.at[b],
            dst_ref=come.at[b],
            send_sem=far_send.at[0, b],
            recv_sem=far_recv.at[0, b],
            device_id={"lon": far},
            device_id_type=MESH,
        )

    def back(b):
        return pltpu.make_async_remote_copy(
            src_ref=heat.at[b],
            dst_ref=heat_in.at[b],
            send_sem=far_send.at[1, b],
            recv_sem=far_recv.at[1, b],
            device_id={"lon": far},
            device_id_type=MESH,
        )

    for b in range(blocks):
        gone[b] = picked(half + b * wide)
        to_far(b).start()
    for b in range(blocks):
        own[b] = picked(b * wide)

    def absorb(b, carry):
        to_far(b).wait()
        cells = own[b] + come[b]
        shift1 = doubled(bias1[...])
        shift2 = doubled(bias2[...])
        for k in range(0, lev, merge):
            raw = jnp.dot(
                w1big[pl.ds(k * hid, merge * hid), :], cells, preferred_element_type=jnp.float32
            )
            for i in range(merge):
                x = raw[i * hid : (i + 1) * hid] + shift1
                first[pl.ds((k + i) * hid, hid), :] = (x + x * jnp.tanh(x)).astype(jnp.bfloat16)
        for k in range(lev):
            part = pl.ds(k * hid, hid)
            x = jnp.dot(w2t[...], first[part, :], preferred_element_type=jnp.float32) + shift2
            second[part, :] = (x + x * jnp.tanh(x)).astype(jnp.bfloat16)
        depth[...] = doubled(start3[...])
        top = jnp.zeros((8, lanes), jnp.float32)
        for g in range(0, gpt, 8):
            top = top + jnp.exp2(FALL * start3[pl.ds(g, 8), :])
        top = doubled(top)

        def one_level(k, above):
            part = pl.ds(k * hid, hid)
            raw = jnp.dot(w3t[...], second[part, :], preferred_element_type=jnp.float32)
            total = jnp.zeros((8, wide), jnp.float32)
            for g in range(0, gpt, chunk):
                at = pl.ds(g, chunk)
                x = raw[g : g + chunk] + doubled(bias3[at, :])
                soft = jnp.maximum(x, jnp.log(1.0 + jnp.exp(jnp.minimum(x, 44.0))))
                here = depth[at, :] + soft
                depth[at, :] = here
                left = jnp.exp2(FALL * here)
                for piece in range(0, chunk, 8):
                    total = total + left[piece : piece + 8]
            heat[b, pl.ds(k, 1), :] = jnp.sum(above - total, axis=0, keepdims=True)
            return total

        above = top
        for k in range(lev):
            above = one_level(k, above)
        back(b).start()
        return carry

    lax.fori_loop(0, blocks, absorb, 0)

    def placed(warm, at):
        high = warm.astype(jnp.bfloat16)
        rest = warm - high.astype(jnp.float32)
        mid = rest.astype(jnp.bfloat16)
        low = (rest - mid.astype(jnp.float32)).astype(jnp.bfloat16)
        out = lax.dot_general(
            jnp.concatenate([high, mid, low], axis=0),
            hot[:, pl.ds(at, wide)],
            (((1,), (1,)), ((), ())),
            preferred_element_type=jnp.float32,
        )
        return out[:lev] + out[lev : 2 * lev] + out[2 * lev :]

    total = placed(heat[0], 0)
    for b in range(1, blocks):
        total = total + placed(heat[b], b * wide)
    grid[...] = total
    for b in range(blocks):
        back(b).wait()
        grid[...] += placed(heat_in[b], half + b * wide)
    for j in range(rows):
        warm = grid[:, j * lanes : (j + 1) * lanes]
        now_out[2, pl.ds(j, lev, stride=rows), :] = temper[j] + warm
    saves[3].start()
    for save in saves:
        save.wait()


def hand_on(prev_ref, now_ref, prev_out, now_out, stage, sem):
    ins, outs = [], []
    for i, (src, dst) in enumerate(((prev_ref, prev_out), (now_ref, now_out))):
        for v in range(src.shape[0]):
            ins.append(pltpu.make_async_copy(src.at[v], stage.at[i, v], sem.at[0, i, v]))
            outs.append(pltpu.make_async_copy(stage.at[i, v], dst.at[v], sem.at[1, i, v]))
    for copy in ins:
        copy.start()
    for copy, out in zip(ins, outs):
        copy.wait()
        out.start()
    for out in outs:
        out.wait()


def body(
    state_prev,
    state_now,
    stride_table,
    filter_len,
    zonal_coef,
    merid_coef,
    filter_coef,
    w_first,
    b_first,
    w_second,
    b_second,
    w_third,
    b_third,
    band_weight,
    sunlit_cols,
    sunlit_count,
):
    nvar, lev, rows, lanes = state_now.shape
    dims = (nvar, lev, rows, lanes, lax.axis_size("lon"), lax.axis_size("lat"))
    hid = w_second.shape[0]
    gpt = w_third.shape[1]
    flat = (nvar, lev * rows, lanes)
    half = sunlit_cols.size // 2
    wide = 2 * lanes
    blocks = half // wide
    tiles = -(-nvar // (lanes // 2 // rows))
    hbm = pl.BlockSpec(memory_space=pltpu.HBM)
    limit = 63 * 1024 * 1024
    f32, bf16 = jnp.float32, jnp.bfloat16
    tile = (lev, lanes)
    shape = jax.ShapeDtypeStruct(flat, f32)
    operands = (
        state_prev.reshape(flat),
        state_now.reshape(flat),
        stride_table,
        filter_len,
        zonal_coef,
        sunlit_count,
        merid_coef[None],
        filter_coef[None],
        w_first,
        b_first[None],
        w_second,
        b_second[None],
        w_third,
        b_third[None],
        band_weight[None],
        sunlit_cols.reshape(1, -1),
    )
    spaces = [pltpu.VMEM] * 2 + [pltpu.SMEM] * 4 + [pltpu.VMEM] * 10
    prev, now = pl.pallas_call(
        functools.partial(kernel, dims, len(operands)),
        out_shape=(shape, shape),
        in_specs=[hbm] * len(operands),
        out_specs=(hbm, hbm),
        scratch_shapes=[space(x.shape, x.dtype) for space, x in zip(spaces, operands)]
        + [
            pltpu.VMEM(flat, f32),
            pltpu.VMEM(flat, f32),
            pltpu.VMEM((nvar, rows + 2) + tile, f32),
            pltpu.VMEM((nvar, rows + 2) + tile, f32),
            pltpu.VMEM((nvar, rows) + tile, f32),
            pltpu.VMEM((rows,) + tile, f32),
            pltpu.VMEM((nvar * lev, rows * lanes), bf16),
            pltpu.VMEM((2, 2, nvar + tiles) + tile, f32),
            pltpu.VMEM((2, 2, nvar + tiles) + tile, f32),
            pltpu.VMEM((2, 2, nvar) + tile, f32),
            pltpu.VMEM((lev * hid, nvar * lev), bf16),
            pltpu.VMEM((hid, hid), bf16),
            pltpu.VMEM((gpt, hid), bf16),
            pltpu.VMEM((hid, lanes), f32),
            pltpu.VMEM((hid, lanes), f32),
            pltpu.VMEM((gpt, lanes), f32),
            pltpu.VMEM((gpt, lanes), f32),
            pltpu.VMEM((lev * hid, wide), bf16),
            pltpu.VMEM((lev * hid, wide), bf16),
            pltpu.VMEM((gpt, wide), f32),
            pltpu.VMEM((blocks, lev, wide), f32),
            pltpu.VMEM((rows * lanes, 2 * half), bf16),
            pltpu.VMEM((blocks, nvar * lev, wide), bf16),
            pltpu.VMEM((blocks, nvar * lev, wide), bf16),
            pltpu.VMEM((blocks, nvar * lev, wide), bf16),
            pltpu.VMEM((blocks, lev, wide), f32),
            pltpu.VMEM((lev, rows * lanes), f32),
            pltpu.SemaphoreType.DMA((len(operands),)),
            pltpu.SemaphoreType.DMA((4,)),
            pltpu.SemaphoreType.DMA((2, 6)),
            pltpu.SemaphoreType.DMA((2, 6)),
            pltpu.SemaphoreType.DMA((2, blocks)),
            pltpu.SemaphoreType.DMA((2, blocks)),
        ],
        compiler_params=pltpu.CompilerParams(
            collective_id=0, has_side_effects=True, vmem_limit_bytes=limit
        ),
    )(*operands)
    prev, now = pl.pallas_call(
        hand_on,
        out_shape=(shape, shape),
        in_specs=[hbm, hbm],
        out_specs=(hbm, hbm),
        scratch_shapes=[pltpu.VMEM((2,) + flat, f32), pltpu.SemaphoreType.DMA((2, 2, nvar))],
        compiler_params=pltpu.CompilerParams(vmem_limit_bytes=limit),
    )(prev, now)
    return prev.reshape(state_prev.shape), now.reshape(state_now.shape)


def solution(mesh):
    field = P(None, None, "lat", "lon")
    in_specs = (
        (field, field, P("lat"), P("lat"), P("lat"))
        + (P(),) * 9
        + (P("lat", "lon", None), P("lat", None))
    )
    return jax.shard_map(
        body, mesh=mesh, in_specs=in_specs, out_specs=(field, field), check_vma=False
    )
```

```python
import functools
import math

import jax
import jax.numpy as jnp
from jax import lax
from jax.experimental import pallas as pl
from jax.experimental.pallas import tpu as pltpu
from jax.sharding import PartitionSpec as P

SMAX = 32
POLAR = 4
MESH = pl.DeviceIdType.MESH
LOG2E = math.log2(math.e)
RATE = 0.15
FALL = -RATE * LOG2E


def column(row, lanes):
    return jnp.transpose(jnp.broadcast_to(row, (lanes, row.shape[1])))


def flipped(weight):
    rows = weight.shape[0]
    eye = (
        lax.broadcasted_iota(jnp.int32, (rows, rows), 0)
        == lax.broadcasted_iota(jnp.int32, (rows, rows), 1)
    ).astype(jnp.float32).astype(jnp.bfloat16)
    return lax.dot_general(
        weight, eye, (((0,), (0,)), ((), ())), preferred_element_type=jnp.float32
    )


def kernel(dims, n_in, *refs):
    operands, refs = refs[:n_in], refs[n_in:]
    prev_hbm, now_hbm, refs = refs[0], refs[1], refs[2:]
    held, refs = refs[:n_in], refs[n_in:]
    (
        prev_ref,
        now_ref,
        stride_ref,
        flen_ref,
        zcoef_ref,
        count_ref,
        mcoef_ref,
        fcoef_ref,
        w1_ref,
        b1_ref,
        w2_ref,
        b2_ref,
        w3_ref,
        b3_ref,
        band_ref,
        list_ref,
    ) = held
    (
        prev_out,
        now_out,
        now0,
        now1,
        prev1,
        temper,
        feats,
        lon_out,
        lon_in,
        lat_in,
        w1big,
        w2t,
        w3t,
        bias1,
        bias2,
        bias3,
        start3,
        first,
        second,
        depth,
        heat,
        hot,
        own,
        gone,
        come,
        heat_in,
        grid,
        load_sem,
        save_sem,
        send_sem,
        recv_sem,
        far_send,
        far_recv,
    ) = refs
    nvar, lev, rows, lanes, n_lon, n_lat = dims
    hid = w2_ref.shape[0]
    gpt = w3_ref.shape[1]
    lon = lax.axis_index("lon")
    lat = lax.axis_index("lat")
    east = lax.rem(lon + 1, n_lon)
    west = lax.rem(lon + n_lon - 1, n_lon)
    far = lax.rem(lon + n_lon // 2, n_lon)
    at_top = lat == 0
    at_end = lat == n_lat - 1
    polar = jnp.logical_or(at_top, at_end)
    pstart = jnp.where(at_top, 0, rows - POLAR)
    per = lanes // 2 // rows
    tiles = -(-nvar // per)

    loads = [
        pltpu.make_async_copy(src, dst, load_sem.at[i])
        for i, (src, dst) in enumerate(zip(operands, held))
    ]
    for i in (1, *range(2, n_in), 0):
        loads[i].start()

    barrier = pltpu.get_barrier_semaphore()
    for peer in (east, west, far):
        pl.semaphore_signal(barrier, inc=1, device_id={"lon": peer}, device_id_type=MESH)

    @pl.when(lat > 0)
    def _():
        pl.semaphore_signal(barrier, inc=1, device_id={"lat": lat - 1}, device_id_type=MESH)

    @pl.when(lat < n_lat - 1)
    def _():
        pl.semaphore_signal(barrier, inc=1, device_id={"lat": lat + 1}, device_id_type=MESH)

    lane = lax.broadcasted_iota(jnp.int32, (lev, lanes), 1)

    def zonal(turn, side, kind):
        part = pl.ds(nvar, tiles) if kind else pl.ds(0, nvar)
        return pltpu.make_async_remote_copy(
            src_ref=lon_out.at[turn, side, part],
            dst_ref=lon_in.at[turn, side, part],
            send_sem=send_sem.at[turn, 2 * kind + side],
            recv_sem=recv_sem.at[turn, 2 * kind + side],
            device_id={"lon": west if side == 0 else east},
            device_id_type=MESH,
        )

    def merid_copy(turn, side, src):
        return pltpu.make_async_remote_copy(
            src_ref=src.at[:, 1 if side == 0 else rows],
            dst_ref=lat_in.at[turn, side],
            send_sem=send_sem.at[turn, 4 + side],
            recv_sem=recv_sem.at[turn, 4 + side],
            device_id={"lat": lat - 1 if side == 0 else lat + 1},
            device_id_type=MESH,
        )

    def send_rows(turn, src):
        @pl.when(lat > 0)
        def _():
            merid_copy(turn, 0, src).start()

        @pl.when(lat < n_lat - 1)
        def _():
            merid_copy(turn, 1, src).start()

    def packed(edges, v, j, x):
        t, place = v // per, (v % per) * rows + j
        turned = pltpu.roll(x, lax.rem(2 * place + 1, lanes), 1)
        edges = list(edges)
        edges[t] = jnp.where(lane // 2 == place, turned, edges[t])
        return tuple(edges)

    no_edges = (jnp.zeros((lev, lanes), jnp.float32),) * tiles

    def send_polar(turn, src):
        for v in range(nvar):
            head = jnp.zeros((lev, lanes), jnp.float32)
            tail = head
            for q in range(POLAR):
                x = src[v, pstart + q + 1]
                turned = pltpu.roll(x, SMAX * q, 1) if q else x
                head = jnp.where(lane // SMAX == q, turned, head)
                tail = jnp.where(lane // SMAX == (q + POLAR - 1) % POLAR, turned, tail)
            lon_out[turn, 0, v] = head
            lon_out[turn, 1, v] = tail
        zonal(turn, 0, 0).start()
        zonal(turn, 1, 0).start()

    def send_early(turn, src):
        send_rows(turn, src)

        @pl.when(polar)
        def _():
            send_polar(turn, src)

    def send_edges(turn):
        for t in range(tiles):
            lon_out[turn, 1, nvar + t] = lon_out[turn, 0, nvar + t]
        zonal(turn, 0, 1).start()
        zonal(turn, 1, 1).start()

    groups = rows // POLAR

    def group_at(i):
        return jnp.where(i == 0, 0, jnp.where(i == 1, groups - 1, i - 1))

    def held_edges(turn):
        return tuple(lon_out[turn, 0, nvar + t] for t in range(tiles))

    def hold_edges(turn, edges):
        for t in range(tiles):
            lon_out[turn, 0, nvar + t] = edges[t]

    def finish(turn, src):
        zonal(turn, 0, 1).wait()
        zonal(turn, 1, 1).wait()

        @pl.when(polar)
        def _():
            zonal(turn, 0, 0).wait()
            zonal(turn, 1, 0).wait()

        @pl.when(lat > 0)
        def _():
            merid_copy(turn, 0, src).wait_send()
            merid_copy(turn, 1, src).wait_recv()
            for v in range(nvar):
                src[v, 0] = lat_in[turn, 1, v]

        @pl.when(lat < n_lat - 1)
        def _():
            merid_copy(turn, 1, src).wait_send()
            merid_copy(turn, 0, src).wait_recv()
            for v in range(nvar):
                src[v, rows + 1] = lat_in[turn, 0, v]

        zero = jnp.zeros((lev, lanes), jnp.float32)

        @pl.when(at_top)
        def _():
            for v in range(nvar):
                src[v, 0] = zero

        @pl.when(at_end)
        def _():
            for v in range(nvar):
                src[v, rows + 1] = zero

    def leap(turn, src, get_prev, put):
        mcoef = column(mcoef_ref[...], lanes)
        fcoef = column(fcoef_ref[...], lanes)
        from_east = lon_in.at[turn, 0]
        from_west = lon_in.at[turn, 1]

        def emit(v, j, x, diff, ends, zu, mv):
            tend = zu * diff - mv * (src[v, j + 2] - src[v, j])
            tend = tend + fcoef * (ends - 2.0 * x)
            old = get_prev(v, j)
            new = old + tend
            put(v, j, x + 0.1 * (old - 2.0 * x + new), new)
            return new

        halos = [
            jnp.where(
                lane % 2 == 0,
                pltpu.roll(from_east[nvar + t], lanes - 1, 1),
                pltpu.roll(from_west[nvar + t], 1, 1),
            )
            for t in range(tiles)
        ]

        def plain(group):
            edges = held_edges(1) if turn == 0 else ()
            for r in range(POLAR):
                j = group * POLAR + r
                zu = -zcoef_ref[j] * src[0, j + 1]
                mv = mcoef * src[1, j + 1]
                for v in range(nvar):
                    x = src[v, j + 1]
                    place = (v % per) * rows + j
                    side = pltpu.roll(halos[v // per], lanes - 1 - 2 * place, 1)
                    plus = jnp.where(lane == lanes - 1, side, pltpu.roll(x, lanes - 1, 1))
                    minus = jnp.where(lane == 0, side, pltpu.roll(x, 1, 1))
                    new = emit(v, j, x, plus - minus, plus + minus, zu, mv)
                    if turn == 0:
                        edges = packed(edges, v, j, new)
            if turn == 0:
                hold_edges(1, edges)

        @pl.when(polar)
        def _():
            for q in range(POLAR):
                j = pstart + q
                s = stride_ref[j]
                m = flen_ref[j]
                inv = 1.0 / jnp.full((lev, lanes), s, jnp.int32).astype(jnp.float32)
                zu = -zcoef_ref[j] * src[0, j + 1]
                mv = mcoef * src[1, j + 1]
                for v in range(nvar):
                    x = src[v, j + 1]
                    side = jnp.where(lane // SMAX == q, from_east[v], from_west[v])
                    if q:
                        side = pltpu.roll(side, lanes - SMAX * q, 1)
                    pair = []
                    for n in (s, m):
                        plus = pltpu.roll(jnp.where(lane < n, side, x), lanes - n, 1)
                        minus = pltpu.roll(jnp.where(lane >= lanes - n, side, x), n, 1)
                        pair.append((plus, minus))
                    diff = (pair[0][0] - pair[0][1]) * inv
                    emit(v, j, x, diff, pair[1][0] + pair[1][1], zu, mv)

        def one_group(i, carry):
            group = group_at(i)
            skip = jnp.logical_or(
                jnp.logical_and(at_top, group == 0), jnp.logical_and(at_end, group == groups - 1)
            )

            @pl.when(jnp.logical_not(skip))
            def _():
                plain(group)

            if turn == 0:

                @pl.when(i == 1)
                def _():
                    send_early(1, now1)

            return carry

        if turn == 0:
            hold_edges(1, no_edges)
        lax.fori_loop(0, groups, one_group, 0)

    def load(i, carry):
        group = group_at(i)
        edges = held_edges(0)
        for r in range(POLAR):
            j = group * POLAR + r
            for v in range(nvar):
                x = now_ref[v, pl.ds(j, lev, stride=rows), :]
                now0[v, j + 1] = x
                edges = packed(edges, v, j, x)
        hold_edges(0, edges)

        @pl.when(i == 1)
        def _():
            send_early(0, now0)

        return carry

    hold_edges(0, no_edges)
    loads[1].wait()
    pl.semaphore_wait(
        barrier, 3 + jnp.where(lat > 0, 1, 0) + jnp.where(lat < n_lat - 1, 1, 0)
    )

    lax.fori_loop(0, groups, load, 0)
    send_edges(0)

    for i in (*range(2, n_in), 0):
        loads[i].wait()

    expand = (
        lax.broadcasted_iota(jnp.int32, (nvar, nvar * lev), 1) // lev
        == lax.broadcasted_iota(jnp.int32, (nvar, nvar * lev), 0)
    ).astype(jnp.float32).astype(jnp.bfloat16)
    spread = lax.dot_general(
        w1_ref[...], expand, (((0,), (0,)), ((), ())), preferred_element_type=jnp.float32
    )
    level = lax.broadcasted_iota(jnp.int32, (hid, nvar * lev), 1) % lev
    for k in range(lev):
        w1big[pl.ds(k * hid, hid), :] = jnp.where(level == k, 0.5 * spread, 0.0).astype(jnp.bfloat16)
    w2t[...] = (0.5 * flipped(w2_ref[...])).astype(jnp.bfloat16)
    w3t[...] = flipped(w3_ref[...]).astype(jnp.bfloat16)
    bias1[...] = column(0.5 * b1_ref[...], lanes)
    bias2[...] = column(0.5 * b2_ref[...], lanes)
    bias3[...] = column(b3_ref[...], lanes)
    start3[...] = column(jnp.log(band_ref[...]) * (-1.0 / RATE), lanes)

    finish(0, now0)

    def put_first(v, j, filtered, new):
        prev1[v, j] = filtered
        now1[v, j + 1] = new

    leap(0, now0, lambda v, j: prev_ref[v, pl.ds(j, lev, stride=rows), :], put_first)
    send_edges(1)

    half = list_ref.shape[1] // 2
    mine = count_ref[0, lon]
    other = count_ref[0, far]
    slot = lax.broadcasted_iota(jnp.int32, (8, half), 1)
    shift = jnp.minimum(other, half - 1)
    moved = pltpu.roll(jnp.broadcast_to(list_ref[:, half:], (8, half)), shift, 1)
    for side, (cols, live) in enumerate(
        (
            (jnp.broadcast_to(list_ref[:, :half], (8, half)), slot < mine),
            (moved, jnp.logical_and(slot >= other, slot < other + mine - half)),
        )
    ):
        cols = jnp.where(live, cols, -1)[:1]
        at = pl.ds(side * half, half)
        lane_hot = (
            lax.broadcasted_iota(jnp.int32, (lanes, half), 0) == cols % lanes
        ).astype(jnp.float32).astype(jnp.bfloat16)
        for j in range(rows):
            row_hot = (cols // lanes == j).astype(jnp.float32).astype(jnp.bfloat16)
            hot[pl.ds(j * lanes, lanes), at] = lane_hot * row_hot

    finish(1, now1)

    def put_second(v, j, filtered, new):
        prev_out[v, pl.ds(j, lev, stride=rows), :] = filtered
        at = pl.ds(pl.multiple_of(j * lanes, lanes), lanes)
        feats[pl.ds(v * lev, lev), at] = new.astype(jnp.bfloat16)
        if v == 2:
            temper[j] = new
        else:
            now_out[v, pl.ds(j, lev, stride=rows), :] = new

    leap(1, now1, lambda v, j: prev1[v, j], put_second)

    saves = [pltpu.make_async_copy(prev_out, prev_hbm, save_sem.at[0])]
    for i, (a, b) in enumerate(((0, 2), (3, nvar), (2, 3))):
        part = pl.ds(a, b - a)
        saves.append(pltpu.make_async_copy(now_out.at[part], now_hbm.at[part], save_sem.at[i + 1]))
    for save in saves[:3]:
        save.start()

    wide = 2 * lanes
    chunk = 16
    blocks = half // wide
    merge = math.gcd(lev, 4)

    def doubled(x):
        return jnp.concatenate([x, x], axis=1)

    def picked(at):
        got = jnp.dot(feats[...], hot[:, pl.ds(at, wide)], preferred_element_type=jnp.float32)
        return got.astype(jnp.bfloat16)

    def to_far(b):
        return pltpu.make_async_remote_copy(
            src_ref=gone.at[b],
            dst_ref=come.at[b],
            send_sem=far_send.at[0, b],
            recv_sem=far_recv.at[0, b],
            device_id={"lon": far},
            device_id_type=MESH,
        )

    def back(b):
        return pltpu.make_async_remote_copy(
            src_ref=heat.at[b],
            dst_ref=heat_in.at[b],
            send_sem=far_send.at[1, b],
            recv_sem=far_recv.at[1, b],
            device_id={"lon": far},
            device_id_type=MESH,
        )

    for b in range(blocks):
        gone[b] = picked(half + b * wide)
        to_far(b).start()
    for b in range(blocks):
        own[b] = picked(b * wide)

    def absorb(b, carry):
        to_far(b).wait()
        cells = own[b] + come[b]
        shift1 = doubled(bias1[...])
        shift2 = doubled(bias2[...])
        for k in range(0, lev, merge):
            raw = jnp.dot(
                w1big[pl.ds(k * hid, merge * hid), :], cells, preferred_element_type=jnp.float32
            )
            for i in range(merge):
                x = raw[i * hid : (i + 1) * hid] + shift1
                first[pl.ds((k + i) * hid, hid), :] = (x + x * jnp.tanh(x)).astype(jnp.bfloat16)
        for k in range(lev):
            part = pl.ds(k * hid, hid)
            x = jnp.dot(w2t[...], first[part, :], preferred_element_type=jnp.float32) + shift2
            second[part, :] = (x + x * jnp.tanh(x)).astype(jnp.bfloat16)
        depth[...] = doubled(start3[...])
        top = jnp.zeros((8, lanes), jnp.float32)
        for g in range(0, gpt, 8):
            top = top + jnp.exp2(FALL * start3[pl.ds(g, 8), :])
        top = doubled(top)

        def one_level(k, above):
            part = pl.ds(k * hid, hid)
            raw = jnp.dot(w3t[...], second[part, :], preferred_element_type=jnp.float32)
            total = jnp.zeros((8, wide), jnp.float32)
            for g in range(0, gpt, chunk):
                at = pl.ds(g, chunk)
                x = raw[g : g + chunk] + doubled(bias3[at, :])
                soft = jnp.maximum(x, jnp.log(1.0 + jnp.exp(jnp.minimum(x, 44.0))))
                here = depth[at, :] + soft
                depth[at, :] = here
                left = jnp.exp2(FALL * here)
                for piece in range(0, chunk, 8):
                    total = total + left[piece : piece + 8]
            heat[b, pl.ds(k, 1), :] = jnp.sum(above - total, axis=0, keepdims=True)
            return total

        above = top
        for k in range(lev):
            above = one_level(k, above)
        back(b).start()
        return carry

    lax.fori_loop(0, blocks, absorb, 0)

    def placed(warm, at):
        high = warm.astype(jnp.bfloat16)
        rest = warm - high.astype(jnp.float32)
        mid = rest.astype(jnp.bfloat16)
        low = (rest - mid.astype(jnp.float32)).astype(jnp.bfloat16)
        out = lax.dot_general(
            jnp.concatenate([high, mid, low], axis=0),
            hot[:, pl.ds(at, wide)],
            (((1,), (1,)), ((), ())),
            preferred_element_type=jnp.float32,
        )
        return out[:lev] + out[lev : 2 * lev] + out[2 * lev :]

    total = placed(heat[0], 0)
    for b in range(1, blocks):
        total = total + placed(heat[b], b * wide)
    grid[...] = total
    for b in range(blocks):
        back(b).wait()
        grid[...] += placed(heat_in[b], half + b * wide)
    for j in range(rows):
        warm = grid[:, j * lanes : (j + 1) * lanes]
        now_out[2, pl.ds(j, lev, stride=rows), :] = temper[j] + warm
    saves[3].start()
    for save in saves:
        save.wait()


def hand_on(prev_ref, now_ref, prev_out, now_out, stage, sem):
    ins, outs = [], []
    for i, (src, dst) in enumerate(((prev_ref, prev_out), (now_ref, now_out))):
        cut = src.shape[0] // 2
        for v, part in enumerate((pl.ds(0, cut), pl.ds(cut, src.shape[0] - cut))):
            ins.append(pltpu.make_async_copy(src.at[part], stage.at[i, part], sem.at[0, i, v]))
            outs.append(pltpu.make_async_copy(stage.at[i, part], dst.at[part], sem.at[1, i, v]))
    for copy in ins:
        copy.start()
    for copy, out in zip(ins, outs):
        copy.wait()
        out.start()
    for out in outs:
        out.wait()


def body(
    state_prev,
    state_now,
    stride_table,
    filter_len,
    zonal_coef,
    merid_coef,
    filter_coef,
    w_first,
    b_first,
    w_second,
    b_second,
    w_third,
    b_third,
    band_weight,
    sunlit_cols,
    sunlit_count,
):
    nvar, lev, rows, lanes = state_now.shape
    dims = (nvar, lev, rows, lanes, lax.axis_size("lon"), lax.axis_size("lat"))
    hid = w_second.shape[0]
    gpt = w_third.shape[1]
    flat = (nvar, lev * rows, lanes)
    half = sunlit_cols.size // 2
    wide = 2 * lanes
    blocks = half // wide
    tiles = -(-nvar // (lanes // 2 // rows))
    hbm = pl.BlockSpec(memory_space=pltpu.HBM)
    limit = 63 * 1024 * 1024
    f32, bf16 = jnp.float32, jnp.bfloat16
    tile = (lev, lanes)
    shape = jax.ShapeDtypeStruct(flat, f32)
    operands = (
        state_prev.reshape(flat),
        state_now.reshape(flat),
        stride_table,
        filter_len,
        zonal_coef,
        sunlit_count,
        merid_coef[None],
        filter_coef[None],
        w_first,
        b_first[None],
        w_second,
        b_second[None],
        w_third,
        b_third[None],
        band_weight[None],
        sunlit_cols.reshape(1, -1),
    )
    spaces = [pltpu.VMEM] * 2 + [pltpu.SMEM] * 4 + [pltpu.VMEM] * 10
    prev, now = pl.pallas_call(
        functools.partial(kernel, dims, len(operands)),
        out_shape=(shape, shape),
        in_specs=[hbm] * len(operands),
        out_specs=(hbm, hbm),
        scratch_shapes=[space(x.shape, x.dtype) for space, x in zip(spaces, operands)]
        + [
            pltpu.VMEM(flat, f32),
            pltpu.VMEM(flat, f32),
            pltpu.VMEM((nvar, rows + 2) + tile, f32),
            pltpu.VMEM((nvar, rows + 2) + tile, f32),
            pltpu.VMEM((nvar, rows) + tile, f32),
            pltpu.VMEM((rows,) + tile, f32),
            pltpu.VMEM((nvar * lev, rows * lanes), bf16),
            pltpu.VMEM((2, 2, nvar + tiles) + tile, f32),
            pltpu.VMEM((2, 2, nvar + tiles) + tile, f32),
            pltpu.VMEM((2, 2, nvar) + tile, f32),
            pltpu.VMEM((lev * hid, nvar * lev), bf16),
            pltpu.VMEM((hid, hid), bf16),
            pltpu.VMEM((gpt, hid), bf16),
            pltpu.VMEM((hid, lanes), f32),
            pltpu.VMEM((hid, lanes), f32),
            pltpu.VMEM((gpt, lanes), f32),
            pltpu.VMEM((gpt, lanes), f32),
            pltpu.VMEM((lev * hid, wide), bf16),
            pltpu.VMEM((lev * hid, wide), bf16),
            pltpu.VMEM((gpt, wide), f32),
            pltpu.VMEM((blocks, lev, wide), f32),
            pltpu.VMEM((rows * lanes, 2 * half), bf16),
            pltpu.VMEM((blocks, nvar * lev, wide), bf16),
            pltpu.VMEM((blocks, nvar * lev, wide), bf16),
            pltpu.VMEM((blocks, nvar * lev, wide), bf16),
            pltpu.VMEM((blocks, lev, wide), f32),
            pltpu.VMEM((lev, rows * lanes), f32),
            pltpu.SemaphoreType.DMA((len(operands),)),
            pltpu.SemaphoreType.DMA((4,)),
            pltpu.SemaphoreType.DMA((2, 6)),
            pltpu.SemaphoreType.DMA((2, 6)),
            pltpu.SemaphoreType.DMA((2, blocks)),
            pltpu.SemaphoreType.DMA((2, blocks)),
        ],
        compiler_params=pltpu.CompilerParams(
            collective_id=0, has_side_effects=True, vmem_limit_bytes=limit
        ),
    )(*operands)
    prev, now = pl.pallas_call(
        hand_on,
        out_shape=(shape, shape),
        in_specs=[hbm, hbm],
        out_specs=(hbm, hbm),
        scratch_shapes=[pltpu.VMEM((2,) + flat, f32), pltpu.SemaphoreType.DMA((2, 2, 2))],
        compiler_params=pltpu.CompilerParams(vmem_limit_bytes=limit),
    )(prev, now)
    return prev.reshape(state_prev.shape), now.reshape(state_now.shape)


def solution(mesh):
    field = P(None, None, "lat", "lon")
    in_specs = (
        (field, field, P("lat"), P("lat"), P("lat"))
        + (P(),) * 9
        + (P("lat", "lon", None), P("lat", None))
    )
    return jax.shard_map(
        body, mesh=mesh, in_specs=in_specs, out_specs=(field, field), check_vma=False
    )
```
